256 devices in a mesh: leaf: 64 (over x, z, core), sub: 4 (over y).
Axes of the slice: x: 4, y: 4, z: 8, core: 2. Of those that a mesh axis runs over, the one named last changes fastest.
Arguments:
- vectors: bfloat16 [16, 524288], P(None, ('leaf', 'sub')), may hold values from -6 to 6
- leaf_size: int32 [8192], P(('leaf', 'sub')), may hold values from 1 to 64, 393216 in all
- leaf_basis: bfloat16 [8192, 4096], P(('leaf', 'sub')), may hold values from -0.75 to 0.75
- near_blocks: bfloat16 [8192, 3, 4096], P(('leaf', 'sub')), may hold values from -0.4375 to 0.4375
- leaf_links: int32 [8192, 8], P(('leaf', 'sub')), may hold values from 0 to 8191, as said below
- leaf_coupling: bfloat16 [8192, 8, 4096], P(('leaf', 'sub')), may hold values from -0.25 to 0.25
- leaf_transfer: bfloat16 [8192, 4096], P(('leaf', 'sub')), may hold values from -0.1875 to 0.1875
- node_transfer: bfloat16 [128, 4096], replicated, may hold values from -0.5 to 0.5
- node_links: int32 [128, 3], replicated, may hold values from 1 to 127, as said below
- node_coupling: bfloat16 [128, 3, 4096], replicated, may hold values from -0.4375 to 0.4375
Outputs:
- product: bfloat16 [16, 524288], P(None, ('leaf', 'sub'))
The draws below stay inside these ranges and needn't reach their ends.
Inputs may be any that keep to these rules, and one draw needn't show every extreme that they name: `leaf_size`: the sizes sum to 393216 and some leaf is full. `leaf_links`: the partners of leaf l lie in its branch (index // 128 equal to l // 128), and in the branch's cyclic order of leaves none is l or adjacent to l. `node_links`: for rows k from 8 on, every partner is a node of k's level that in the level's cyclic order is neither k nor adjacent to k; rows under 8 are not read.
All inputs are finite; a program needn't handle non-finite values. No bound on the sum of `leaf_size` on one device may be relied on, other than what follows from the above.
Results may differ from the reference program's by a relative error of at most 0.0055.
Values may be sent and summed in bfloat16 or wider, within the bound.
No kernel may reach another device: no remote copies, remote signals or barrier semaphores. Data moves between devices by JAX's collectives and lax.ppermute only.
A program may use at most 64 MiB of HBM per device.

```python
import math
import jax
import jax.numpy as jnp
import numpy as np
from jax import lax

LEAF_PTS = 64
RANK = 64
COLUMNS = 16
LEAF_LINKS = 8
NODE_LINKS = 3
BRANCHES = 64
BRANCH_LEAVES = 128
LEAVES = 8192
POINTS = 524288
NODES = 128


def draw_leaf_links(key, part):
    key = jax.random.fold_in(key, 11)
    leaves = jnp.arange(LEAVES, dtype=jnp.int32)[:, None]
    offset = jax.random.randint(key, (LEAVES, LEAF_LINKS), 2, BRANCH_LEAVES - 1, dtype=jnp.int32)
    branch_base = leaves // BRANCH_LEAVES * BRANCH_LEAVES
    return branch_base + (leaves % BRANCH_LEAVES + offset) % BRANCH_LEAVES


def draw_node_links(key, part):
    key = jax.random.fold_in(key, 23)
    node_ids = jnp.arange(NODES, dtype=jnp.int32)[:, None]
    level_size = jnp.ones_like(node_ids)
    for exponent in range(1, 16):
        level_size = jnp.where(node_ids >= 2 ** exponent, 2 ** exponent, level_size)
    offset = jax.random.randint(key, (NODES, NODE_LINKS), 2, jnp.maximum(level_size - 1, 3), dtype=jnp.int32)
    return level_size + (node_ids - level_size + offset) % level_size


def shard_levels(stream_key, dims, pieces, least, top_value):
    loudness = 1.0
    for dim, blocks in pieces:
        heights = jax.random.uniform(jax.random.fold_in(jax.random.fold_in(stream_key, 6), dim), (blocks,), jnp.float32, least / len(pieces), top_value / len(pieces))
        loudness = loudness * jnp.repeat(jnp.exp(heights), dims[dim] // blocks).reshape((-1,) + (1,) * (len(dims) - 1 - dim))
    return loudness


def length_profile(count, total, bound, skew):
    weights = [(1 << 20) // math.isqrt(rank ** skew) + 1 for rank in range(2, count + 1)]
    rest, holding = total - bound - (count - 1), [1] * (count - 1)
    while rest > 0:
        movable = [i for i in range(count - 1) if holding[i] < bound]
        whole, remaining = sum([weights[i] for i in movable]), rest
        for i in movable:
            more = min(bound - holding[i], max(1, remaining * weights[i] // whole), rest)
            holding[i] = holding[i] + more
            rest = rest - more
    return np.array([bound] + holding)


def ragged_sizes(own_key, amount, total, most, lean):
    if amount == 2:
        one = jax.random.randint(own_key, (), max(1, total - most), min(most, total - 1) + 1)
        return jnp.stack([one, total - one])
    lengths = jnp.asarray(length_profile(amount, total, most, lean), jnp.int32)
    couples = (amount - 1) // 2
    donor, taker = lengths[1:1 + 2 * couples:2], lengths[2:2 + 2 * couples:2]
    slack = jnp.minimum(donor - 1, most - taker)
    passed = jax.random.randint(jax.random.fold_in(own_key, 1), (couples,), 0, 1 << 20) % (slack + 1)
    lengths = lengths.at[1:1 + 2 * couples:2].set(donor - passed).at[2:2 + 2 * couples:2].set(taker + passed)
    return lengths[jax.random.permutation(jax.random.fold_in(own_key, 2), amount)]


def gaussian(key, shape, scale, bound, split=(), held_as=jnp.bfloat16):
    level = shard_levels(key, shape, split, -0.22, 0.18) if split else 1.0
    array = jax.random.normal(key, shape, jnp.float32) * scale * level
    return jnp.minimum(jnp.maximum(array, -bound), bound).astype(held_as)


def setup_inputs(seed: int = 0) -> dict:
    splits = jax.random.split(jax.random.key(seed), 11)
    return {
        "vectors": gaussian(splits[0], (COLUMNS, POINTS), 1.0, 6.0, ((1, 256),)),
        "leaf_size": ragged_sizes(splits[1], LEAVES, 3 * POINTS // 4, LEAF_PTS, 0).astype(jnp.int32),
        "leaf_basis": gaussian(splits[2], (LEAVES, LEAF_PTS * RANK), LEAF_PTS ** -0.5, 0.75, ((0, 256),)),
        "near_blocks": gaussian(splits[3], (LEAVES, 3, LEAF_PTS * LEAF_PTS), (3 * LEAF_PTS) ** -0.5, 0.4375, ((0, 256),)),
        "leaf_links": draw_leaf_links(jax.random.fold_in(splits[10], 71), 0),
        "leaf_coupling": gaussian(splits[5], (LEAVES, LEAF_LINKS, RANK * RANK), (LEAF_LINKS * RANK) ** -0.5, 0.25, ((0, 256),)),
        "leaf_transfer": gaussian(splits[6], (LEAVES, RANK * RANK), (16 * RANK) ** -0.5, 0.1875, ((0, 256),)),
        "node_transfer": gaussian(splits[7], (NODES, RANK * RANK), (2 * RANK) ** -0.5, 0.5),
        "node_links": draw_node_links(jax.random.fold_in(splits[10], 71), 0),
        "node_coupling": gaussian(splits[9], (NODES, NODE_LINKS, RANK * RANK), (NODE_LINKS * RANK) ** -0.5, 0.4375),
    }


highest = lax.Precision.HIGHEST


def node_upward(branch_rows, node_transfer):
    level_map = {BRANCHES: branch_rows}
    level_size = BRANCHES
    while level_size > 8:
        parent_size = level_size // 2
        children = level_map[level_size].reshape(parent_size, 2, COLUMNS, RANK)
        matrices = node_transfer[level_size:2 * level_size].astype(jnp.float32).reshape(parent_size, 2, RANK, RANK)
        level_map[parent_size] = jnp.einsum("nckr,ncrs->nks", children, matrices, precision=highest)
        level_size = parent_size
    return level_map


def reference(vectors, leaf_size, leaf_basis, near_blocks, leaf_links, leaf_coupling, leaf_transfer, node_transfer, node_links, node_coupling):
    present = jnp.arange(LEAF_PTS, dtype=jnp.int32)[None, :] < leaf_size[:, None]
    masked = jnp.where(present.reshape(1, POINTS), vectors, jnp.zeros_like(vectors))
    padded = jnp.pad(masked, ((0, 0), (LEAF_PTS, LEAF_PTS)))
    span = BRANCH_LEAVES * LEAF_PTS

    def leaf_coeffs(branch):
        first_leaf = branch * BRANCH_LEAVES
        points_view = lax.dynamic_slice_in_dim(masked, first_leaf * LEAF_PTS, span, 1).reshape(COLUMNS, BRANCH_LEAVES, LEAF_PTS)
        basis_mats = lax.dynamic_slice_in_dim(leaf_basis, first_leaf, BRANCH_LEAVES, 0).reshape(BRANCH_LEAVES, LEAF_PTS, RANK)
        coeffs = jnp.einsum("klp,lpr->lkr", points_view.astype(jnp.float32), basis_mats.astype(jnp.float32)).astype(jnp.bfloat16)
        transfers = lax.dynamic_slice_in_dim(leaf_transfer, first_leaf, BRANCH_LEAVES, 0).reshape(BRANCH_LEAVES, RANK, RANK)
        summed = jnp.einsum("lkr,lrs->ks", coeffs.astype(jnp.float32), transfers.astype(jnp.float32))
        return coeffs, summed

    all_coeffs, branch_rows = lax.map(leaf_coeffs, jnp.arange(BRANCHES, dtype=jnp.int32))

    level_map = node_upward(branch_rows, node_transfer)
    ascending = []
    level_size = 8
    while level_size <= BRANCHES:
        ascending.append(level_size)
        level_size = level_size * 2
    node_table = jnp.concatenate([jnp.zeros((8, COLUMNS, RANK), jnp.float32)] + [level_map[size_now] for size_now in ascending], axis=0)
    downward = jnp.zeros((8, COLUMNS, RANK), jnp.float32)
    for position, level_size in enumerate(ascending):
        partners = node_links[level_size:2 * level_size]
        gathered = node_table[partners]
        matrices = node_coupling[level_size:2 * level_size].astype(jnp.float32).reshape(level_size, NODE_LINKS, RANK, RANK)
        coupled = jnp.einsum("nckr,ncrs->nks", gathered, matrices, precision=highest)
        if position == 0:
            downward = coupled
        else:
            inherited = jnp.repeat(downward, 2, axis=0)
            transfer = node_transfer[level_size:2 * level_size].astype(jnp.float32).reshape(level_size, RANK, RANK)
            downward = coupled + jnp.einsum("nks,nrs->nkr", inherited, transfer, precision=highest)
    branch_down = downward.astype(jnp.bfloat16)

    def leaf_output(branch):
        first_leaf = branch * BRANCH_LEAVES
        window = lax.dynamic_slice_in_dim(padded, first_leaf * LEAF_PTS, span + 2 * LEAF_PTS, 1)
        blocks = lax.dynamic_slice_in_dim(near_blocks, first_leaf, BRANCH_LEAVES, 0).reshape(BRANCH_LEAVES, 3, LEAF_PTS, LEAF_PTS).astype(jnp.float32)
        near_field = jnp.zeros((COLUMNS, BRANCH_LEAVES, LEAF_PTS), jnp.float32)
        for neighbour in range(3):
            shifted = window[:, neighbour * LEAF_PTS:neighbour * LEAF_PTS + span].reshape(COLUMNS, BRANCH_LEAVES, LEAF_PTS)
            near_field = near_field + jnp.einsum("lpq,klq->klp", blocks[:, neighbour], shifted.astype(jnp.float32))
        partners = lax.dynamic_slice_in_dim(leaf_links, first_leaf, BRANCH_LEAVES, 0) - first_leaf
        picked = jnp.take(all_coeffs[branch], partners, axis=0).astype(jnp.float32)
        coupling = lax.dynamic_slice_in_dim(leaf_coupling, first_leaf, BRANCH_LEAVES, 0).reshape(BRANCH_LEAVES, LEAF_LINKS, RANK, RANK).astype(jnp.float32)
        linked = jnp.einsum("lckr,lcrs->lks", picked, coupling)
        transfers = lax.dynamic_slice_in_dim(leaf_transfer, first_leaf, BRANCH_LEAVES, 0).reshape(BRANCH_LEAVES, RANK, RANK).astype(jnp.float32)
        far_field = (linked + jnp.einsum("ks,lrs->lkr", branch_down[branch].astype(jnp.float32), transfers)).astype(jnp.bfloat16)
        basis_mats = lax.dynamic_slice_in_dim(leaf_basis, first_leaf, BRANCH_LEAVES, 0).reshape(BRANCH_LEAVES, LEAF_PTS, RANK).astype(jnp.float32)
        expanded = jnp.einsum("lkr,lpr->klp", far_field.astype(jnp.float32), basis_mats)
        sizes_here = lax.dynamic_slice_in_dim(leaf_size, first_leaf, BRANCH_LEAVES, 0)
        used = jnp.arange(LEAF_PTS, dtype=jnp.int32)[None, :] < sizes_here[:, None]
        combined = jnp.where(used[None], near_field + expanded, jnp.zeros_like(expanded))
        return combined.astype(jnp.bfloat16).reshape(COLUMNS, span)

    outputs = lax.map(leaf_output, jnp.arange(BRANCHES, dtype=jnp.int32))
    return jnp.transpose(outputs, (1, 0, 2)).reshape(COLUMNS, POINTS)
```

```python
import jax
import jax.numpy as jnp
from jax import lax
from jax.experimental import pallas as pl
from jax.experimental.pallas import tpu as pltpu
from jax.sharding import PartitionSpec as P

F32, BF16, I32 = jnp.float32, jnp.bfloat16, jnp.int32
TILES = 16
COEFF = 16 * 128
PAYLOAD = 19 * 128


def iota(shape, dim):
    return lax.broadcasted_iota(I32, shape, dim)


def dot(a, b):
    return jnp.dot(a, b, preferred_element_type=F32)


def dot_t(a, b):
    return lax.dot_general(a, b, (((1,), (1,)), ((), ())), preferred_element_type=F32)


def swap(x):
    return pltpu.roll(x, 64, 1)


def low_half(rows):
    return iota((rows, 128), 1) < 64


def tile(ref, j):
    return ref[:, 128 * j : 128 * j + 128]


def pieces(x):
    high = x.astype(BF16)
    return high, (x - high.astype(F32)).astype(BF16)


def split_map():
    row = iota((512, 128), 0)
    rank = row & 63
    target = (rank & 1) * 256 + (rank >> 1) * 8 + (row >> 6) - iota((512, 128), 1)
    return jnp.concatenate(
        [jnp.where(target == 128 * q, 1.0, 0.0).astype(BF16) for q in range(4)], axis=1
    )


def present(size_ref, j):
    lane = iota((16, 128), 1)
    limit = jnp.where(lane < 64, size_ref[2 * j], size_ref[2 * j + 1])
    return (lane & 63) < limit


def upward_kernel(size_ref, x_ref, basis_ref, transfer_ref, pay_ref, masked_ref, cross_ref, map_ref):
    lo = low_half(16)
    for j in range(TILES):
        kept = jnp.where(present(size_ref, j), tile(x_ref, j).astype(F32), 0.0)
        masked_ref[:, 128 * j : 128 * j + 128] = kept.astype(BF16)
    map_ref[...] = split_map()
    points = jnp.concatenate([masked_ref[:, 512 * g : 512 * g + 512] for g in range(4)], axis=0)
    spread = dot(points, map_ref[...]).astype(BF16)
    member = iota((16, 256), 1) & 7
    picks = [jnp.where(member == m, 1.0, 0.0).astype(BF16) for m in range(8)]
    for g in range(4):
        halves = [spread[16 * g : 16 * g + 16, 256 * h : 256 * h + 256] for h in range(2)]
        rows = jnp.concatenate([halves[h] * picks[m] for m in range(8) for h in range(2)], axis=0)
        out = dot(rows, basis_ref[g])
        for q in range(4):
            a0, a1, b0, b1 = [out[64 * q + 16 * n : 64 * q + 16 * n + 16] for n in range(4)]
            coeff = jnp.where(lo, a0 + swap(a1), swap(b0) + b1)
            j = 4 * g + q
            pay_ref[:, 128 * j : 128 * j + 128] = coeff.astype(BF16)
    coeffs = jnp.concatenate([pay_ref[:, 512 * g : 512 * g + 512] for g in range(4)], axis=0)
    spread = dot(coeffs, map_ref[...]).astype(BF16)
    total = jnp.zeros((32, 128), F32)
    for g in range(4):
        rows = jnp.concatenate(
            [spread[16 * g : 16 * g + 16, 256 * h : 256 * h + 256] for h in range(2)], axis=0
        )
        total = total + dot(rows, transfer_ref[g])
    share = jnp.where(lo, total[:16] + swap(total[16:]), swap(total[:16]) + total[16:])
    high = share.astype(BF16).astype(F32)
    pay_ref[:, COEFF : COEFF + 128] = jnp.where(lo, high, share - high).astype(BF16)
    first, last = tile(masked_ref, 0), tile(masked_ref, 15)
    pay_ref[:, COEFF + 128 : COEFF + 256] = first
    pay_ref[:, COEFF + 256 : COEFF + 384] = last
    at_start = lax.axis_index("sub") == 0
    cross_ref[...] = jnp.where(at_start, first.astype(F32), last.astype(F32)).astype(BF16)


def parity_rows(raw, count):
    even = (iota((count, 128), 0) & 1) == 0
    return jnp.where(low_half(count) == even, raw, swap(raw))


def prepare_kernel(
    masked_ref, near_ref, basis_ref, transfer_ref, nodes_ref, coupling_ref,
    field_ref, edge_ref, basis_out, transfer_out, nodes_out, coupled_out, map_out,
    sides_ref, near_f32, sums_ref, coupling_buf, coupling_sem,
):
    branch = lax.axis_index("leaf")
    own = [64 + branch, 32 + (branch >> 1), 16 + (branch >> 2), 8 + (branch >> 3)]
    copies = [
        pltpu.make_async_copy(coupling_ref.at[own[n]], coupling_buf.at[n], coupling_sem.at[n])
        for n in range(4)
    ]
    for copy in copies:
        copy.start()
    lo = low_half(16)
    map_out[...] = split_map()
    row, col = iota((512, 256), 0), iota((512, 256), 1)
    plain = jnp.where(((row >> 6) == (col & 7)) & (((row & 63) >> 1) == (col >> 3)), 1.0, 0.0).astype(BF16)
    member = (iota((512, 128), 0) >> 6) & 1
    own_half = (member == 0) == (iota((512, 128), 1) < 64)
    for g in range(4):
        for source, target in ((basis_ref, basis_out), (transfer_ref, transfer_out)):
            rows = parity_rows(dot(plain, source[g]), 512)
            target[512 * g : 512 * g + 512] = jnp.where(own_half, rows, 0.0).astype(BF16)

    def node_group(g, _):
        rows = parity_rows(dot(plain, nodes_ref[g + 2]), 512).astype(BF16)
        nodes_out[pl.ds(pl.multiple_of(g * 512, 512), 512), :] = rows
        return 0

    lax.fori_loop(0, 14, node_group, 0)

    sides_ref[0] = jnp.zeros((32, 128), BF16)
    sides_ref[33] = jnp.zeros((32, 128), BF16)
    for j in range(TILES):
        x = tile(masked_ref, j).astype(F32)
        y = swap(x)
        sides_ref[2 * j + 1, 0:16, :] = jnp.where(lo, x, 0.0).astype(BF16)
        sides_ref[2 * j + 1, 16:32, :] = jnp.where(lo, 0.0, y).astype(BF16)
        sides_ref[2 * j + 2, 0:16, :] = jnp.where(lo, y, 0.0).astype(BF16)
        sides_ref[2 * j + 2, 16:32, :] = jnp.where(lo, 0.0, x).astype(BF16)
    near_f32[...] = jnp.zeros((2, 128, 128), F32)
    which = iota((32, 128), 1) & 3

    def stage(slot, get):
        for i in range(32):
            near_f32[slot, 4 * i : 4 * i + 3, :] = get(i).astype(F32)
        return near_f32[slot].astype(BF16)

    def near_leaf(leaf, slot):
        block = stage(slot, lambda i: near_ref[leaf, i])
        out = dot_t(sides_ref[pl.ds(leaf, 3)].reshape(96, 128), block)
        near = jnp.where(which == 0, out[:32], jnp.where(which == 1, out[32:64], out[64:]))
        high, low = pieces(near)
        start = pl.multiple_of(leaf * 16, 16)
        for h in range(2):
            sums_ref[0, pl.ds(start, 16), 128 * h : 128 * h + 128] = high[16 * h : 16 * h + 16]
            sums_ref[1, pl.ds(start, 16), 128 * h : 128 * h + 128] = low[16 * h : 16 * h + 16]
        return block

    row, col = iota((64, 128), 0), iota((64, 128), 1)
    half = iota((64, 128), 1) < 64

    def edge(block, s):
        pick = jnp.where(((row >> 1) == (col >> 2)) & ((col & 3) == s), 1.0, 0.0).astype(BF16)
        return parity_rows(dot(pick, block), 64)

    zeros = jnp.zeros((64, 128), BF16)
    edge_ref[0, 0:64, :] = jnp.where(half, 0.0, edge(near_leaf(0, 0), 0)).astype(BF16)
    edge_ref[0, 64:128, :] = zeros
    edge_ref[1, 0:64, :] = zeros
    edge_ref[1, 64:128, :] = jnp.where(half, edge(near_leaf(31, 1), 2), 0.0).astype(BF16)

    def near_pair(n, _):
        near_leaf(2 * n + 1, 0)
        near_leaf(2 * n + 2, 1)
        return 0

    lax.fori_loop(0, 15, near_pair, 0)
    row, col = iota((256, 128), 0), iota((256, 128), 1)
    gather = jnp.where((col & 63) == ((row >> 7) + 2 * ((row & 127) >> 2)), 1.0, 0.0)
    gather = jnp.where((row & 3) == 3, 0.0, gather).astype(BF16)
    fields = dot(sums_ref[0], gather) + dot(sums_ref[1], gather)
    for j in range(TILES):
        field_ref[:, 128 * j : 128 * j + 128] = jnp.where(
            lo, fields[32 * j : 32 * j + 16], fields[32 * j + 16 : 32 * j + 32]
        )

    for copy in copies:
        copy.wait()
    row, col = iota((256, 128), 0), iota((256, 128), 1)
    order = jnp.where(((row >> 6) == (col & 3)) & (((row & 63) >> 1) == (col >> 2)), 1.0, 0.0).astype(BF16)

    def node(n):
        return nodes_out[pl.ds(pl.multiple_of((own[n] - 16) * 64, 64), 64), :]

    def both(x):
        x = x.astype(F32)
        return jnp.concatenate([jnp.where(half, x, 0.0), jnp.where(half, 0.0, x)], axis=0).astype(BF16)

    chain = [None]
    carried = (node(0), None)
    for n in range(1, 4):
        high, low = carried
        parts = [both(high)] + ([both(low)] if low is not None else [])
        chain.append(jnp.concatenate(parts, axis=0))
        if n < 3:
            below = node(n)
            longer = dot(high[:, :64], below)
            if low is not None:
                longer = longer + dot(low[:, :64], below)
            carried = pieces(longer)
    lo256 = low_half(256)
    for n in range(4):
        block = stage(n & 1, lambda i: coupling_buf[n, i])
        if n == 0:
            rows = jnp.where(lo256, parity_rows(dot(order, block), 256), 0.0)
        else:
            both_parts = dot_t(block, chain[n])
            summed = both_parts[:, :128]
            if n > 1:
                summed = summed + both_parts[:, 128:]
            high, low = pieces(summed)
            rows = jnp.where(
                lo256, parity_rows(dot(order, high), 256), parity_rows(dot(order, low), 256)
            )
        coupled_out[256 * n : 256 * n + 256, :] = rows.astype(BF16)


def message_kernel(own_ref, one_ref, two_ref, three_ref, out_ref):
    total = (
        own_ref[...].astype(F32) + one_ref[...].astype(F32)
        + two_ref[...].astype(F32) + three_ref[...].astype(F32)
    )
    total = total + swap(total)
    packed = jnp.where(low_half(8), total[:8], total[8:]).astype(BF16)
    for n in range(64):
        out_ref[n] = packed


def downward_kernel(
    size_ref, links_ref, node_links_ref, own_ref, one_ref, two_ref, three_ref, cross_ref, message_ref,
    coupling_ref, field_ref, edge_ref, basis_ref, transfer_ref, nodes_ref, coupled_ref, map_ref,
    out_ref,
    coeff_ref, picked_ref, spread_ref, linked_ref, table_ref,
):
    branch, sub = lax.axis_index("leaf"), lax.axis_index("sub")
    lo = low_half(16)
    lo8 = low_half(8)
    lo32 = low_half(32)

    pairs = []
    for q in range(32):
        one, two = message_ref[2 * q].astype(F32), message_ref[2 * q + 1].astype(F32)
        one_s, two_s = swap(one), swap(two)
        pairs.append(
            jnp.concatenate([jnp.where(lo8, one, two_s), jnp.where(lo8, one_s, two)], axis=0).astype(BF16)
        )
        first = jnp.concatenate([jnp.where(lo8, one, one_s), jnp.where(lo8, one_s, one)], axis=0)
        second = jnp.concatenate([jnp.where(lo8, two, two_s), jnp.where(lo8, two_s, two)], axis=0)
        zeros = jnp.zeros((16, 128), BF16)
        table_ref[64 + 2 * q] = jnp.concatenate([first.astype(BF16), zeros], axis=0)
        table_ref[65 + 2 * q] = jnp.concatenate([second.astype(BF16), zeros], axis=0)

    def weights(q):
        return nodes_ref[128 * (q - 8) : 128 * (q - 8) + 128, :]

    size = 32
    while size >= 8:
        parents = []
        for q in range(size, 2 * size):
            a = dot(pairs[q - size], weights(q))
            if size < 32:
                a = a[:16] + a[16:]
            high, low = pieces(a)
            parents.append(jnp.concatenate([high, low], axis=0))
            table_ref[q] = parents[-1]
        pairs = [
            jnp.where(lo32, parents[2 * q].astype(F32), parents[2 * q + 1].astype(F32)).astype(BF16)
            for q in range(size // 2)
        ]
        size = size // 2
    sources = []
    for n in range(4):
        own = (64 >> n) + (branch >> n)
        a, b, c = [table_ref[node_links_ref[own, m]].astype(F32) for m in range(3)]
        sources += [jnp.where(lo32, a, b).astype(BF16), jnp.where(lo32, c, 0.0).astype(BF16)]
    down = dot(jnp.concatenate(sources, axis=1), coupled_ref[...])
    down = down[:16] + down[16:]
    down = (down + swap(down)).astype(BF16)
    inherited = dot_t(down, transfer_ref[...])

    for d, ref in enumerate((own_ref, one_ref, two_ref, three_ref)):
        for j in range(TILES):
            x = tile(ref, j).astype(F32)
            y = swap(x)
            coeff_ref[32 * d + 2 * j] = jnp.where(lo, x, y).astype(BF16)
            coeff_ref[32 * d + 2 * j + 1] = jnp.where(lo, y, x).astype(BF16)
    for leaf in range(32):
        for c in range(4):
            ends = []
            for m in range(2):
                link = links_ref[leaf, 2 * c + m] & 127
                slot = ((sub - (link >> 5)) & 3) * 32 + (link & 31)
                ends.append(coeff_ref[slot].astype(F32))
            picked_ref[16 * leaf : 16 * leaf + 16, 128 * c : 128 * c + 128] = jnp.where(
                lo, ends[0], ends[1]
            ).astype(BF16)
    spread_ref[...] = dot(picked_ref[...], map_ref[...]).astype(BF16)
    for j in range(TILES):
        outs = []
        for leaf in (2 * j, 2 * j + 1):
            rows = spread_ref[16 * leaf : 16 * leaf + 16, :]
            outs.append(
                dot(jnp.concatenate([rows[:, :256], rows[:, 256:]], axis=0), coupling_ref[leaf])
            )
        a, b = outs
        linked_ref[:, 128 * j : 128 * j + 128] = jnp.where(
            lo, a[:16] + swap(a[16:]), swap(b[:16]) + b[16:]
        )

    left = jnp.where(sub == 0, cross_ref[...].astype(F32), tile(one_ref, 18).astype(F32)).astype(BF16)
    right = jnp.where(sub == 3, cross_ref[...].astype(F32), tile(three_ref, 17).astype(F32)).astype(BF16)
    for j in range(TILES):
        far = (linked_ref[:, 128 * j : 128 * j + 128] + inherited[:, 128 * j : 128 * j + 128]).astype(BF16)
        out = dot_t(far, basis_ref[128 * j : 128 * j + 128, :]) + tile(field_ref, j)
        if j == 0:
            out = out + dot_t(left, edge_ref[0])
        if j == 15:
            out = out + dot_t(right, edge_ref[1])
        out_ref[:, 128 * j : 128 * j + 128] = jnp.where(present(size_ref, j), out, 0.0).astype(BF16)


VMEM = pl.BlockSpec(memory_space=pltpu.VMEM)
SMEM = pl.BlockSpec(memory_space=pltpu.SMEM)
ANY = pl.BlockSpec(memory_space=pl.ANY)


def params(mib):
    return pltpu.CompilerParams(vmem_limit_bytes=mib << 20)


def cost(flops, size):
    return pl.CostEstimate(flops=flops, bytes_accessed=size, transcendentals=0)


def shape(dims, dtype=BF16):
    return jax.ShapeDtypeStruct(dims, dtype)


def grouped(table):
    rows = table.shape[0]
    return table.reshape(rows // 8, 8, 32, 128).transpose(0, 2, 1, 3).reshape(rows // 8, 256, 128)


def body(
    vectors, leaf_size, leaf_basis, near_blocks, leaf_links, leaf_coupling, leaf_transfer,
    node_transfer, node_links, node_coupling,
):
    basis, transfer, nodes = grouped(leaf_basis), grouped(leaf_transfer), grouped(node_transfer)
    coupling = leaf_coupling.reshape(32, 8, 32, 128).transpose(0, 2, 1, 3).reshape(32, 256, 128)
    near = near_blocks.reshape(32, 3, 32, 128).transpose(0, 2, 1, 3)
    node_coupled = node_coupling.reshape(128, 3, 32, 128).transpose(0, 2, 1, 3)

    payload, masked, cross = pl.pallas_call(
        upward_kernel,
        out_shape=[shape((16, PAYLOAD)), shape((16, 2048)), shape((16, 128))],
        in_specs=[SMEM, VMEM, VMEM, VMEM],
        out_specs=[VMEM, VMEM, VMEM],
        scratch_shapes=[pltpu.VMEM((512, 512), BF16)],
        compiler_params=params(16),
        cost_estimate=cost(10**8, 10**6),
        name="upward",
    )(leaf_size, vectors, basis, transfer)

    others = [
        lax.ppermute(payload, "sub", [(s, (s + d) % 4) for s in range(4)]) for d in (1, 2, 3)
    ]
    branches = lax.axis_size("leaf")
    routes = [(4 * b + 3, 4 * b + 4) for b in range(branches - 1)]
    routes += [(4 * b, 4 * b - 1) for b in range(1, branches)]
    cross = lax.ppermute(cross, ("leaf", "sub"), routes)

    field, edge, basis_p, transfer_p, nodes_p, coupled, split = pl.pallas_call(
        prepare_kernel,
        out_shape=[
            shape((16, 2048), F32), shape((2, 128, 128)), shape((2048, 128)), shape((2048, 128)),
            shape((56 * 128, 128)), shape((1024, 128)), shape((512, 512)),
        ],
        in_specs=[VMEM, VMEM, VMEM, VMEM, VMEM, ANY],
        out_specs=[VMEM] * 7,
        scratch_shapes=[
            pltpu.VMEM((34, 32, 128), BF16),
            pltpu.VMEM((2, 128, 128), F32),
            pltpu.VMEM((2, 512, 256), BF16),
            pltpu.VMEM((4, 32, 3, 128), BF16),
            pltpu.SemaphoreType.DMA((4,)),
        ],
        compiler_params=params(24),
        cost_estimate=cost(3 * 10**9, 6 * 10**6),
        name="prepare",
    )(masked, near, basis, transfer, nodes, node_coupled)

    share = pl.BlockSpec((16, 128), lambda n: (0, 16))
    messages = pl.pallas_call(
        message_kernel,
        grid=(1,),
        out_shape=shape((64, 8, 128)),
        in_specs=[share] * 4,
        out_specs=pl.BlockSpec((64, 8, 128), lambda n: (0, 0, 0)),
        compiler_params=params(4),
        name="message",
    )(payload, *others)
    messages = lax.all_to_all(messages, "leaf", 0, 0)

    return pl.pallas_call(
        downward_kernel,
        out_shape=shape((16, 2048)),
        in_specs=[SMEM] * 3 + [VMEM] * 14,
        out_specs=VMEM,
        scratch_shapes=[
            pltpu.VMEM((128, 16, 128), BF16),
            pltpu.VMEM((512, 512), BF16),
            pltpu.VMEM((512, 512), BF16),
            pltpu.VMEM((16, 2048), F32),
            pltpu.VMEM((128, 32, 128), BF16),
        ],
        compiler_params=params(24),
        name="downward",
    )(
        leaf_size, leaf_links, node_links, payload, *others, cross, messages,
        coupling, field, edge, basis_p, transfer_p, nodes_p, coupled, split,
    )


def solution(mesh):
    split = ("leaf", "sub")
    placed = (
        P(None, split), P(split), P(split, None), P(split, None, None), P(split, None),
        P(split, None, None), P(split, None), P(), P(), P(),
    )
    return jax.shard_map(
        body, mesh=mesh, in_specs=placed, out_specs=P(None, split), check_vma=False
    )
```

```python
import jax
import jax.numpy as jnp
from jax import lax
from jax.experimental import pallas as pl
from jax.experimental.pallas import tpu as pltpu
from jax.sharding import PartitionSpec as P

F32, BF16, I32 = jnp.float32, jnp.bfloat16, jnp.int32
TILES = 16
COEFF = 16 * 128
PAYLOAD = 19 * 128


def iota(shape, dim):
    return lax.broadcasted_iota(I32, shape, dim)


def dot(a, b):
    return jnp.dot(a, b, preferred_element_type=F32)


def dot_t(a, b):
    return lax.dot_general(a, b, (((1,), (1,)), ((), ())), preferred_element_type=F32)


def swap(x):
    return pltpu.roll(x, 64, 1)


def low_half(rows):
    return iota((rows, 128), 1) < 64


def tile(ref, j):
    return ref[:, 128 * j : 128 * j + 128]


def pieces(x):
    high = x.astype(BF16)
    return high, (x - high.astype(F32)).astype(BF16)


def split_map():
    row = iota((512, 128), 0)
    rank = row & 63
    target = (rank & 1) * 256 + (rank >> 1) * 8 + (row >> 6) - iota((512, 128), 1)
    return jnp.concatenate(
        [jnp.where(target == 128 * q, 1.0, 0.0).astype(BF16) for q in range(4)], axis=1
    )


def present(size_ref, j):
    lane = iota((16, 128), 1)
    limit = jnp.where(lane < 64, size_ref[2 * j], size_ref[2 * j + 1])
    return (lane & 63) < limit


def kept(size_ref, x_ref, j):
    return jnp.where(present(size_ref, j), tile(x_ref, j).astype(F32), 0.0)


def start_all(sems, pairs):
    copies = [pltpu.make_async_copy(a, b, sems.at[n]) for n, (a, b) in enumerate(pairs)]
    for copy in copies:
        copy.start()
    return copies


def upward_kernel(
    size_hbm, x_hbm, basis_hbm, transfer_hbm, pay_ref,
    size_ref, x_ref, basis_ref, transfer_ref, masked_ref, map_ref, sems,
):
    copies = start_all(
        sems,
        [(x_hbm, x_ref), (size_hbm, size_ref), (basis_hbm, basis_ref), (transfer_hbm, transfer_ref)],
    )
    lo = low_half(16)
    map_ref[...] = split_map()
    copies[0].wait()
    copies[1].wait()
    for j in range(TILES):
        masked_ref[:, 128 * j : 128 * j + 128] = kept(size_ref, x_ref, j).astype(BF16)
    points = jnp.concatenate([masked_ref[:, 512 * g : 512 * g + 512] for g in range(4)], axis=0)
    spread = dot(points, map_ref[...]).astype(BF16)
    member = iota((16, 256), 1) & 7
    picks = [jnp.where(member == m, 1.0, 0.0).astype(BF16) for m in range(8)]
    copies[2].wait()
    for g in range(4):
        halves = [spread[16 * g : 16 * g + 16, 256 * h : 256 * h + 256] for h in range(2)]
        rows = jnp.concatenate([halves[h] * picks[m] for m in range(8) for h in range(2)], axis=0)
        out = dot(rows, basis_ref[g])
        for q in range(4):
            a0, a1, b0, b1 = [out[64 * q + 16 * n : 64 * q + 16 * n + 16] for n in range(4)]
            coeff = jnp.where(lo, a0 + swap(a1), swap(b0) + b1)
            j = 4 * g + q
            pay_ref[:, 128 * j : 128 * j + 128] = coeff.astype(BF16)
    coeffs = jnp.concatenate([pay_ref[:, 512 * g : 512 * g + 512] for g in range(4)], axis=0)
    spread = dot(coeffs, map_ref[...]).astype(BF16)
    copies[3].wait()
    total = jnp.zeros((32, 128), F32)
    for g in range(4):
        rows = jnp.concatenate(
            [spread[16 * g : 16 * g + 16, 256 * h : 256 * h + 256] for h in range(2)], axis=0
        )
        total = total + dot(rows, transfer_ref[g])
    share = jnp.where(lo, total[:16] + swap(total[16:]), swap(total[:16]) + total[16:])
    high = share.astype(BF16).astype(F32)
    pay_ref[:, COEFF : COEFF + 128] = jnp.where(lo, high, share - high).astype(BF16)
    pay_ref[:, COEFF + 128 : COEFF + 256] = tile(masked_ref, 0)
    pay_ref[:, COEFF + 256 : COEFF + 384] = tile(masked_ref, 15)


def parity_rows(raw, count):
    even = (iota((count, 128), 0) & 1) == 0
    return jnp.where(low_half(count) == even, raw, swap(raw))


def plain_order():
    row, col = iota((512, 256), 0), iota((512, 256), 1)
    return jnp.where(((row >> 6) == (col & 7)) & (((row & 63) >> 1) == (col >> 3)), 1.0, 0.0).astype(BF16)


def near_kernel(
    size_hbm, x_hbm, near_hbm, basis_hbm, transfer_hbm, _, field_hbm, edge_hbm, basis_out, transfer_out,
    size_ref, x_ref, near_ref, basis_ref, transfer_ref,
    masked_ref, blocks_ref, field_ref, edge_ref, basis_rows, transfer_rows, sems, out_sems,
):
    copies = start_all(
        sems,
        [
            (basis_hbm, basis_ref), (transfer_hbm, transfer_ref), (x_hbm, x_ref), (size_hbm, size_ref),
            (near_hbm, near_ref),
        ],
    )
    plain = plain_order()
    own_half = (((iota((512, 128), 0) >> 6) & 1) == 0) == (iota((512, 128), 1) < 64)
    outs = []
    for n, (source, rows, target) in enumerate(
        ((basis_ref, basis_rows, basis_out), (transfer_ref, transfer_rows, transfer_out))
    ):
        copies[n].wait()
        for g in range(4):
            full = parity_rows(dot(plain, source[g]), 512)
            rows[512 * g : 512 * g + 512] = jnp.where(own_half, full, 0.0).astype(BF16)
        outs.append(pltpu.make_async_copy(rows, target, out_sems.at[n]))
        outs[-1].start()
    for n in (2, 3, 4):
        copies[n].wait()
    masked_ref[:, 0:128] = jnp.zeros((16, 128), BF16)
    masked_ref[:, 17 * 128 : 18 * 128] = jnp.zeros((16, 128), BF16)
    for j in range(TILES):
        masked_ref[:, 128 * j + 128 : 128 * j + 256] = kept(size_ref, x_ref, j).astype(BF16)
    lo = low_half(16)
    half = low_half(64)
    for g in range(4):
        for s in range(3):
            blocks_ref[s] = parity_rows(dot(plain, near_ref[s, g]), 512)
        for q in range(4):
            j = 4 * g + q
            a = [blocks_ref[s, 128 * q : 128 * q + 64, :] for s in range(3)]
            b = [blocks_ref[s, 128 * q + 64 : 128 * q + 128, :] for s in range(3)]
            inner = jnp.concatenate([jnp.where(half, a[1], a[2]), jnp.where(half, b[0], b[1])], axis=0)
            outer = jnp.concatenate([jnp.where(half, 0.0, a[0]), jnp.where(half, b[2], 0.0)], axis=0)
            outer = outer.astype(BF16)
            if j in (0, 15):
                edge_ref[j // 15] = outer
            around = jnp.where(lo, tile(masked_ref, j + 2).astype(F32), tile(masked_ref, j).astype(F32))
            field_ref[:, 128 * j : 128 * j + 128] = dot_t(
                tile(masked_ref, j + 1), inner.astype(BF16)
            ) + dot_t(around.astype(BF16), outer)
    for n, (source, target) in enumerate(((field_ref, field_hbm), (edge_ref, edge_hbm))):
        outs.append(pltpu.make_async_copy(source, target, out_sems.at[2 + n]))
        outs[-1].start()
    for copy in outs:
        copy.wait()


def message_kernel(own_ref, one_ref, two_ref, three_ref, _, out_ref, cross_ref):
    share = slice(COEFF, COEFF + 128)
    total = (
        own_ref[:, share].astype(F32) + one_ref[:, share].astype(F32)
        + two_ref[:, share].astype(F32) + three_ref[:, share].astype(F32)
    )
    total = total + swap(total)
    packed = jnp.where(low_half(8), total[:8], total[8:]).astype(BF16)
    for n in range(64):
        out_ref[n] = packed
    at_start = lax.axis_index("sub") == 0
    cross_ref[...] = jnp.where(
        at_start, tile(own_ref, 17).astype(F32), tile(own_ref, 18).astype(F32)
    ).astype(BF16)


def nodes_kernel(
    nodes_hbm, coupling_hbm, _, nodes_out, coupled_out,
    nodes_ref, coupling_ref, rows_ref, coupled_ref, sems, out_sems,
):
    branch = lax.axis_index("leaf")
    own = [64 + branch, 32 + (branch >> 1), 16 + (branch >> 2), 8 + (branch >> 3)]
    copies = start_all(
        sems,
        [(nodes_hbm, nodes_ref)] + [(coupling_hbm.at[:, own[n] >> 3], coupling_ref.at[n]) for n in range(4)],
    )
    plain = plain_order()
    copies[0].wait()
    for g in range(2, 16):
        start = 512 * (g - 2)
        rows_ref[start : start + 512, :] = parity_rows(dot(plain, nodes_ref[g]), 512).astype(BF16)
    outs = [pltpu.make_async_copy(rows_ref, nodes_out, out_sems.at[0])]
    outs[0].start()

    half = low_half(64)
    row, col = iota((64, 256), 0), iota((64, 256), 1)

    def node(n):
        return rows_ref[pl.ds(pl.multiple_of((own[n] - 16) * 64, 64), 64), :]

    def low_only(x):
        return jnp.where(half, x.astype(F32), 0.0).astype(BF16)

    carried = [None, (node(0), None)]
    for n in (1, 2):
        high, low = carried[n]
        longer = dot(high[:, :64], node(n))
        if low is not None:
            longer = longer + dot(low[:, :64], node(n))
        carried.append(pieces(longer))
    for copy in copies[1:]:
        copy.wait()
    lo192 = low_half(192)
    for n in range(4):
        pick = jnp.where(((row >> 1) == (col >> 3)) & ((col & 7) == (own[n] & 7)), 1.0, 0.0).astype(BF16)
        blocks = jnp.concatenate(
            [parity_rows(dot(pick, coupling_ref[n, c]), 64) for c in range(3)], axis=0
        )
        if n == 0:
            rows = jnp.where(lo192, blocks, 0.0)
        else:
            blocks = jnp.where(lo192, blocks, 0.0).astype(BF16)
            high, low = carried[n]
            full = dot_t(blocks, jnp.concatenate([high, high], axis=0))
            if low is not None:
                full = full + dot_t(blocks, jnp.concatenate([low, low], axis=0))
            upper = full.astype(BF16).astype(F32)
            rows = jnp.where(lo192, upper, full - upper)
        coupled_ref[256 * n : 256 * n + 192, :] = rows.astype(BF16)
        coupled_ref[256 * n + 192 : 256 * n + 256, :] = jnp.zeros((64, 128), BF16)
    outs.append(pltpu.make_async_copy(coupled_ref, coupled_out, out_sems.at[1]))
    outs[1].start()
    for copy in outs:
        copy.wait()


def couple_kernel(
    links_hbm, coupling_hbm, own_ref, one_ref, two_ref, three_ref, _, linked_hbm,
    links_ref, coupling_ref, coeff_ref, picked_ref, spread_ref, linked_ref, sems, out_sem,
):
    copies = start_all(
        sems,
        [(links_hbm, links_ref)]
        + [(coupling_hbm.at[pl.ds(8 * n, 8)], coupling_ref.at[pl.ds(8 * n, 8)]) for n in range(4)],
    )
    sub = lax.axis_index("sub")
    lo = low_half(16)
    split = split_map()
    for d, ref in enumerate((own_ref, one_ref, two_ref, three_ref)):
        for j in range(TILES):
            x = tile(ref, j).astype(F32)
            y = swap(x)
            coeff_ref[32 * d + 2 * j] = jnp.where(lo, x, y).astype(BF16)
            coeff_ref[32 * d + 2 * j + 1] = jnp.where(lo, y, x).astype(BF16)
    copies[0].wait()
    for leaf in range(32):
        for c in range(4):
            ends = []
            for m in range(2):
                link = links_ref[2 * c + m, leaf] & 127
                slot = ((sub - (link >> 5)) & 3) * 32 + (link & 31)
                ends.append(coeff_ref[slot].astype(F32))
            picked_ref[16 * leaf : 16 * leaf + 16, 128 * c : 128 * c + 128] = jnp.where(
                lo, ends[0], ends[1]
            ).astype(BF16)
    spread_ref[...] = dot(picked_ref[...], split).astype(BF16)
    for j in range(TILES):
        if j % 4 == 0:
            copies[1 + j // 4].wait()
        outs = []
        for leaf in (2 * j, 2 * j + 1):
            rows = spread_ref[16 * leaf : 16 * leaf + 16, :]
            outs.append(
                dot(jnp.concatenate([rows[:, :256], rows[:, 256:]], axis=0), coupling_ref[leaf])
            )
        a, b = outs
        linked_ref[:, 128 * j : 128 * j + 128] = jnp.where(
            lo, a[:16] + swap(a[16:]), swap(b[:16]) + b[16:]
        )
    copy = pltpu.make_async_copy(linked_ref, linked_hbm, out_sem)
    copy.start()
    copy.wait()


def downward_kernel(
    size_hbm, node_links_hbm, one_ref, three_ref, cross_ref, message_ref,
    linked_hbm, field_hbm, edge_hbm, basis_hbm, transfer_hbm, nodes_hbm, coupled_hbm,
    out_ref,
    size_ref, node_links_ref, linked_ref, field_ref, edge_ref, basis_ref, transfer_ref, nodes_ref,
    coupled_ref, table_ref, sems,
):
    copies = start_all(
        sems,
        [
            (nodes_hbm.at[pl.ds(24 * 128, 32 * 128)], nodes_ref.at[pl.ds(24 * 128, 32 * 128)]),
            (nodes_hbm.at[pl.ds(0, 24 * 128)], nodes_ref.at[pl.ds(0, 24 * 128)]),
            (node_links_hbm, node_links_ref), (coupled_hbm, coupled_ref), (transfer_hbm, transfer_ref),
            (basis_hbm, basis_ref), (linked_hbm, linked_ref), (field_hbm, field_ref), (edge_hbm, edge_ref),
            (size_hbm, size_ref),
        ],
    )
    branch, sub = lax.axis_index("leaf"), lax.axis_index("sub")
    lo = low_half(16)
    lo8 = low_half(8)
    lo32 = low_half(32)

    pairs = []
    for q in range(32):
        one, two = message_ref[2 * q].astype(F32), message_ref[2 * q + 1].astype(F32)
        one_s, two_s = swap(one), swap(two)
        pairs.append(
            jnp.concatenate([jnp.where(lo8, one, two_s), jnp.where(lo8, one_s, two)], axis=0).astype(BF16)
        )
        first = jnp.concatenate([jnp.where(lo8, one, one_s), jnp.where(lo8, one_s, one)], axis=0)
        second = jnp.concatenate([jnp.where(lo8, two, two_s), jnp.where(lo8, two_s, two)], axis=0)
        zeros = jnp.zeros((16, 128), BF16)
        table_ref[64 + 2 * q] = jnp.concatenate([first.astype(BF16), zeros], axis=0)
        table_ref[65 + 2 * q] = jnp.concatenate([second.astype(BF16), zeros], axis=0)

    def weights(q):
        return nodes_ref[128 * (q - 8) : 128 * (q - 8) + 128, :]

    size = 32
    copies[0].wait()
    while size >= 8:
        parents = []
        for q in range(size, 2 * size):
            a = dot(pairs[q - size], weights(q))
            if size < 32:
                a = a[:16] + a[16:]
            high, low = pieces(a)
            parents.append(jnp.concatenate([high, low], axis=0))
            table_ref[q] = parents[-1]
        if size == 32:
            copies[1].wait()
        pairs = [
            jnp.where(lo32, parents[2 * q].astype(F32), parents[2 * q + 1].astype(F32)).astype(BF16)
            for q in range(size // 2)
        ]
        size = size // 2
    copies[2].wait()
    sources = []
    for n in range(4):
        own = (64 >> n) + (branch >> n)
        a, b, c = [table_ref[node_links_ref[m, own]].astype(F32) for m in range(3)]
        sources += [jnp.where(lo32, a, b).astype(BF16), jnp.where(lo32, c, 0.0).astype(BF16)]
    copies[3].wait()
    down = dot(jnp.concatenate(sources, axis=1), coupled_ref[...])
    down = down[:16] + down[16:]
    down = (down + swap(down)).astype(BF16)
    for copy in copies[4:]:
        copy.wait()
    inherited = dot_t(down, transfer_ref[...])

    left = jnp.where(sub == 0, cross_ref[...].astype(F32), tile(one_ref, 18).astype(F32))
    left = jnp.where(lo, 0.0, left).astype(BF16)
    right = jnp.where(sub == 3, cross_ref[...].astype(F32), tile(three_ref, 17).astype(F32))
    right = jnp.where(lo, right, 0.0).astype(BF16)
    for j in range(TILES):
        far = (tile(linked_ref, j) + inherited[:, 128 * j : 128 * j + 128]).astype(BF16)
        out = dot_t(far, basis_ref[128 * j : 128 * j + 128, :]) + tile(field_ref, j)
        if j == 0:
            out = out + dot_t(left, edge_ref[0])
        if j == 15:
            out = out + dot_t(right, edge_ref[1])
        out_ref[:, 128 * j : 128 * j + 128] = jnp.where(present(size_ref, j), out, 0.0).astype(BF16)


VMEM = pl.BlockSpec(memory_space=pltpu.VMEM)
HBM = pl.BlockSpec(memory_space=pltpu.HBM)
ANY = pl.BlockSpec(memory_space=pl.ANY)


def params(mib):
    return pltpu.CompilerParams(vmem_limit_bytes=mib << 20)


def cost(flops, size):
    return pl.CostEstimate(flops=flops, bytes_accessed=size, transcendentals=0)


def shape(dims, dtype=BF16):
    return jax.ShapeDtypeStruct(dims, dtype)


def grouped(table):
    lead, rows = table.shape[:-2], table.shape[-2]
    table = jnp.swapaxes(table.reshape(*lead, rows // 8, 8, 32, 128), -3, -2)
    return table.reshape(*lead, rows // 8, 256, 128)


def dma(count):
    return pltpu.SemaphoreType.DMA((count,))


def body(
    vectors, leaf_size, leaf_basis, near_blocks, leaf_links, leaf_coupling, leaf_transfer,
    node_transfer, node_links, node_coupling,
):
    basis, transfer, nodes = grouped(leaf_basis), grouped(leaf_transfer), grouped(node_transfer)
    coupling = grouped(leaf_coupling)[:, 0]
    near = grouped(near_blocks.transpose(1, 0, 2))
    node_coupled = grouped(node_coupling.transpose(1, 0, 2))

    payload = pl.pallas_call(
        upward_kernel,
        out_shape=shape((16, PAYLOAD)),
        in_specs=[HBM] * 4,
        out_specs=VMEM,
        scratch_shapes=[
            pltpu.SMEM((32,), I32),
            pltpu.VMEM((16, 2048), BF16),
            pltpu.VMEM((4, 256, 128), BF16),
            pltpu.VMEM((4, 256, 128), BF16),
            pltpu.VMEM((16, 2048), BF16),
            pltpu.VMEM((512, 512), BF16),
            dma(4),
        ],
        compiler_params=params(60),
        cost_estimate=cost(10**8, 10**6),
        name="upward",
    )(leaf_size, vectors, basis, transfer)

    others = [
        lax.ppermute(payload, "sub", [(s, (s + d) % 4) for s in range(4)]) for d in (1, 2, 3)
    ]

    field, edge, basis_p, transfer_p = pl.pallas_call(
        near_kernel,
        out_shape=[
            shape((16, 2048), F32), shape((2, 128, 128)), shape((2048, 128)), shape((2048, 128)),
        ],
        in_specs=[HBM] * 5 + [ANY],
        out_specs=[HBM] * 4,
        scratch_shapes=[
            pltpu.SMEM((32,), I32),
            pltpu.VMEM((16, 2048), BF16),
            pltpu.VMEM((3, 4, 256, 128), BF16),
            pltpu.VMEM((4, 256, 128), BF16),
            pltpu.VMEM((4, 256, 128), BF16),
            pltpu.VMEM((16, 18 * 128), BF16),
            pltpu.VMEM((3, 512, 128), F32),
            pltpu.VMEM((16, 2048), F32),
            pltpu.VMEM((2, 128, 128), BF16),
            pltpu.VMEM((2048, 128), BF16),
            pltpu.VMEM((2048, 128), BF16),
            dma(5),
            dma(4),
        ],
        compiler_params=params(60),
        cost_estimate=cost(10**9, 3 * 10**6),
        name="near",
    )(leaf_size, vectors, near, basis, transfer, payload)

    messages, cross = pl.pallas_call(
        message_kernel,
        out_shape=[shape((64, 8, 128)), shape((16, 128))],
        in_specs=[VMEM] * 4 + [ANY],
        out_specs=[VMEM] * 2,
        compiler_params=params(60),
        name="message",
    )(payload, *others, edge)
    summed = lax.all_to_all(messages, "leaf", 0, 0)

    branches = lax.axis_size("leaf")
    routes = [(4 * b + 3, 4 * b + 4) for b in range(branches - 1)]
    routes += [(4 * b, 4 * b - 1) for b in range(1, branches)]
    cross = lax.ppermute(cross, ("leaf", "sub"), routes)

    nodes_p, coupled = pl.pallas_call(
        nodes_kernel,
        out_shape=[shape((56 * 128, 128)), shape((1024, 128))],
        in_specs=[HBM] * 2 + [ANY],
        out_specs=[HBM] * 2,
        scratch_shapes=[
            pltpu.VMEM((16, 256, 128), BF16),
            pltpu.VMEM((4, 3, 256, 128), BF16),
            pltpu.VMEM((56 * 128, 128), BF16),
            pltpu.VMEM((1024, 128), BF16),
            dma(5),
            dma(2),
        ],
        compiler_params=params(60),
        cost_estimate=cost(10**9, 3 * 10**6),
        name="nodes",
    )(nodes, node_coupled, messages)

    linked = pl.pallas_call(
        couple_kernel,
        out_shape=shape((16, 2048), F32),
        in_specs=[HBM] * 2 + [VMEM] * 4 + [ANY],
        out_specs=HBM,
        scratch_shapes=[
            pltpu.SMEM((8, 32), I32),
            pltpu.VMEM((32, 256, 128), BF16),
            pltpu.VMEM((128, 16, 128), BF16),
            pltpu.VMEM((512, 512), BF16),
            pltpu.VMEM((512, 512), BF16),
            pltpu.VMEM((16, 2048), F32),
            dma(5),
            pltpu.SemaphoreType.DMA,
        ],
        compiler_params=params(60),
        cost_estimate=cost(10**9, 3 * 10**6),
        name="couple",
    )(leaf_links.T, coupling, payload, *others, messages)

    return pl.pallas_call(
        downward_kernel,
        out_shape=shape((16, 2048)),
        in_specs=[HBM] * 2 + [VMEM] * 4 + [HBM] * 7,
        out_specs=VMEM,
        scratch_shapes=[
            pltpu.SMEM((32,), I32),
            pltpu.SMEM((3, 128), I32),
            pltpu.VMEM((16, 2048), F32),
            pltpu.VMEM((16, 2048), F32),
            pltpu.VMEM((2, 128, 128), BF16),
            pltpu.VMEM((2048, 128), BF16),
            pltpu.VMEM((2048, 128), BF16),
            pltpu.VMEM((56 * 128, 128), BF16),
            pltpu.VMEM((1024, 128), BF16),
            pltpu.VMEM((128, 32, 128), BF16),
            dma(10),
        ],
        compiler_params=params(60),
        name="downward",
    )(
        leaf_size, node_links.T, others[0], others[2], cross, summed,
        linked, field, edge, basis_p, transfer_p, nodes_p, coupled,
    )


def solution(mesh):
    split = ("leaf", "sub")
    placed = (
        P(None, split), P(split), P(split, None), P(split, None, None), P(split, None),
        P(split, None, None), P(split, None), P(), P(), P(),
    )
    return jax.shard_map(
        body, mesh=mesh, in_specs=placed, out_specs=P(None, split), check_vma=False
    )
```

```python
import jax
import jax.numpy as jnp
from jax import lax
from jax.experimental import pallas as pl
from jax.experimental.pallas import tpu as pltpu
from jax.sharding import PartitionSpec as P

F32, BF16, I32 = jnp.float32, jnp.bfloat16, jnp.int32
TILES = 16
COEFF = 16 * 128
PAYLOAD = 19 * 128


def iota(shape, dim):
    return lax.broadcasted_iota(I32, shape, dim)


def dot(a, b):
    return jnp.dot(a, b, preferred_element_type=F32)


def dot_t(a, b):
    return lax.dot_general(a, b, (((1,), (1,)), ((), ())), preferred_element_type=F32)


def swap(x):
    return pltpu.roll(x, 64, 1)


def low_half(rows):
    return iota((rows, 128), 1) < 64


def tile(ref, j):
    return ref[:, 128 * j : 128 * j + 128]


def pieces(x):
    high = x.astype(BF16)
    return high, (x - high.astype(F32)).astype(BF16)


def split_map():
    row = iota((512, 128), 0)
    rank = row & 63
    target = (rank & 1) * 256 + (rank >> 1) * 8 + (row >> 6) - iota((512, 128), 1)
    return jnp.concatenate(
        [jnp.where(target == 128 * q, 1.0, 0.0).astype(BF16) for q in range(4)], axis=1
    )


def group_map():
    row, col = iota((256, 256), 0), iota((256, 256), 1)
    return jnp.where(col == (row & 31) * 8 + (row >> 5), 1.0, 0.0).astype(BF16)


def plain_rows(raw, rows_ref):
    count = raw.shape[0]
    lo = low_half(count)
    other = swap(raw)
    rows_ref[pl.ds(0, count, stride=2), :] = jnp.where(lo, raw, other)
    rows_ref[pl.ds(1, count, stride=2), :] = jnp.where(lo, other, raw)


def present(size_ref, j):
    lane = iota((16, 128), 1)
    limit = jnp.where(lane < 64, size_ref[2 * j], size_ref[2 * j + 1])
    return (lane & 63) < limit


def kept(size_ref, x_ref, j):
    return jnp.where(present(size_ref, j), tile(x_ref, j).astype(F32), 0.0)


def start_all(sems, pairs):
    copies = [pltpu.make_async_copy(a, b, sems.at[n]) for n, (a, b) in enumerate(pairs)]
    for copy in copies:
        copy.start()
    return copies


def upward_kernel(
    size_hbm, x_hbm, basis_hbm, transfer_hbm, pay_ref, cross_ref,
    size_ref, x_ref, basis_ref, transfer_ref, masked_ref, map_ref, sems,
):
    copies = start_all(
        sems,
        [(x_hbm, x_ref), (size_hbm, size_ref), (basis_hbm, basis_ref), (transfer_hbm, transfer_ref)],
    )
    lo = low_half(16)
    map_ref[...] = split_map()
    copies[0].wait()
    copies[1].wait()
    for j in range(TILES):
        masked_ref[:, 128 * j : 128 * j + 128] = kept(size_ref, x_ref, j).astype(BF16)
    points = jnp.concatenate([masked_ref[:, 512 * g : 512 * g + 512] for g in range(4)], axis=0)
    spread = dot(points, map_ref[...]).astype(BF16)
    member = iota((16, 256), 1) & 7
    picks = [jnp.where(member == m, 1.0, 0.0).astype(BF16) for m in range(8)]
    copies[2].wait()
    for g in range(4):
        halves = [spread[16 * g : 16 * g + 16, 256 * h : 256 * h + 256] for h in range(2)]
        rows = jnp.concatenate([halves[h] * picks[m] for m in range(8) for h in range(2)], axis=0)
        out = dot(rows, basis_ref[g])
        for q in range(4):
            a0, a1, b0, b1 = [out[64 * q + 16 * n : 64 * q + 16 * n + 16] for n in range(4)]
            coeff = jnp.where(lo, a0 + swap(a1), swap(b0) + b1)
            j = 4 * g + q
            pay_ref[:, 128 * j : 128 * j + 128] = coeff.astype(BF16)
    coeffs = jnp.concatenate([pay_ref[:, 512 * g : 512 * g + 512] for g in range(4)], axis=0)
    spread = dot(coeffs, map_ref[...]).astype(BF16)
    copies[3].wait()
    total = jnp.zeros((32, 128), F32)
    for g in range(4):
        rows = jnp.concatenate(
            [spread[16 * g : 16 * g + 16, 256 * h : 256 * h + 256] for h in range(2)], axis=0
        )
        total = total + dot(rows, transfer_ref[g])
    share = jnp.where(lo, total[:16] + swap(total[16:]), swap(total[:16]) + total[16:])
    packed = jnp.where(low_half(8), share[:8], share[8:])
    high = packed.astype(BF16).astype(F32)
    pay_ref[:, COEFF : COEFF + 128] = jnp.concatenate([high, packed - high], axis=0).astype(BF16)
    first, last = tile(masked_ref, 0), tile(masked_ref, 15)
    pay_ref[:, COEFF + 128 : COEFF + 256] = first
    pay_ref[:, COEFF + 256 : COEFF + 384] = last
    cross_ref[...] = jnp.where(lax.axis_index("sub") == 0, first, last)


def near_kernel(
    size_hbm, x_hbm, near_hbm, basis_hbm, transfer_hbm, pay_ref,
    field_ref, basis_rows, transfer_rows, share_ref,
    size_ref, x_ref, near_ref, basis_ref, transfer_ref, masked_ref, raw_ref, sems,
):
    copies = start_all(
        sems,
        [
            (basis_hbm, basis_ref), (transfer_hbm, transfer_ref), (x_hbm, x_ref), (size_hbm, size_ref),
            (near_hbm, near_ref),
        ],
    )
    share_ref[...] = tile(pay_ref, 16)
    collect = group_map()
    half = low_half(64)
    copies[0].wait()
    copies[1].wait()
    for g in range(4):
        raw = dot(collect, jnp.concatenate([basis_ref[g], transfer_ref[g]], axis=1))
        for n, rows in enumerate((basis_rows, transfer_rows)):
            plain_rows(raw[:, 128 * n : 128 * n + 128], raw_ref.at[n])
            for q in range(4):
                pair = [raw_ref[n, 128 * q + 64 * m : 128 * q + 64 * m + 64, :] for m in range(2)]
                start = 256 * g + 64 * q
                rows[start : start + 64, :] = jnp.where(half, pair[0], pair[1]).astype(BF16)
    for copy in copies[2:]:
        copy.wait()
    masked_ref[:, 0:128] = jnp.zeros((16, 128), BF16)
    masked_ref[:, 17 * 128 : 18 * 128] = jnp.zeros((16, 128), BF16)
    for j in range(TILES):
        masked_ref[:, 128 * j + 128 : 128 * j + 256] = kept(size_ref, x_ref, j).astype(BF16)
    lo = low_half(16)
    for pair in range(2):
        for s in range(3):
            raw = dot(
                collect, jnp.concatenate([near_ref[s, 2 * pair], near_ref[s, 2 * pair + 1]], axis=1)
            )
            for n in range(2):
                plain_rows(raw[:, 128 * n : 128 * n + 128], raw_ref.at[3 * n + s])
        for q in range(8):
            j = 8 * pair + q
            at = 128 * (q % 4)
            a = [raw_ref[3 * (q // 4) + s, at : at + 64, :] for s in range(3)]
            b = [raw_ref[3 * (q // 4) + s, at + 64 : at + 128, :] for s in range(3)]
            inner = jnp.concatenate([jnp.where(half, a[1], a[2]), jnp.where(half, b[0], b[1])], axis=0)
            outer = jnp.concatenate([jnp.where(half, 0.0, a[0]), jnp.where(half, b[2], 0.0)], axis=0)
            outer = outer.astype(BF16)
            if j in (0, 15):
                start = 1024 + 128 * (j // 15)
                transfer_rows[start : start + 128, :] = outer
            around = jnp.where(lo, tile(masked_ref, j + 2), tile(masked_ref, j))
            field_ref[:, 128 * j : 128 * j + 128] = dot_t(
                jnp.concatenate([tile(masked_ref, j + 1), around], axis=1),
                jnp.concatenate([inner.astype(BF16), outer], axis=1),
            )


def message_kernel(share_ref, one_ref, two_ref, three_ref, out_ref):
    total = share_ref[...].astype(F32)
    for ref in (one_ref, two_ref, three_ref):
        total = total + tile(ref, 16).astype(F32)
    packed = (total[:8] + total[8:]).astype(BF16)
    for n in range(64):
        out_ref[n] = packed


def middle_kernel(
    nodes_hbm, node_coupling_hbm, links_hbm, coupling_hbm, own_ref, one_ref, two_ref, three_ref,
    rows_ref, coupled_ref, linked_ref,
    links_ref, nodes_ref, node_coupling_ref, coupling_ref,
    raw_ref, coeff_ref, picked_ref, spread_ref, sems,
):
    branch = lax.axis_index("leaf")
    own = [64 + branch, 32 + (branch >> 1), 16 + (branch >> 2), 8 + (branch >> 3)]
    sources = (own_ref, one_ref, two_ref, three_ref)
    copies = start_all(
        sems,
        [(nodes_hbm.at[pl.ds(2, 14)], nodes_ref)]
        + [(node_coupling_hbm.at[:, own[n] >> 3], node_coupling_ref.at[n]) for n in range(4)]
        + [(links_hbm, links_ref)]
        + [(coupling_hbm.at[pl.ds(8 * n, 8)], coupling_ref.at[pl.ds(8 * n, 8)]) for n in range(4)],
    )
    collect = group_map()
    split = split_map()
    copies[0].wait()
    for g in range(0, 14, 2):
        raw = dot(collect, jnp.concatenate([nodes_ref[g], nodes_ref[g + 1]], axis=1))
        for n in range(2):
            plain_rows(raw[:, 128 * n : 128 * n + 128], raw_ref.at[n])
            rows_ref[512 * (g + n) : 512 * (g + n) + 512, :] = raw_ref[n].astype(BF16)

    half = low_half(64)
    row, col = iota((64, 256), 0), iota((64, 256), 1)
    even = (iota((64, 128), 0) & 1) == 0

    def node(n):
        return rows_ref[pl.ds(pl.multiple_of((own[n] - 16) * 64, 64), 64), :]

    carried = [None, (node(0), None)]
    for n in (1, 2):
        high, low = carried[n]
        longer = dot(high[:, :64], node(n))
        if low is not None:
            longer = longer + dot(low[:, :64], node(n))
        carried.append(pieces(longer))
    for copy in copies[1:5]:
        copy.wait()
    lo192 = low_half(192)
    for n in range(4):
        pick = jnp.where(((row >> 1) == (col >> 3)) & ((col & 7) == (own[n] & 7)), 1.0, 0.0).astype(BF16)
        blocks = []
        for c in range(3):
            raw = dot(pick, node_coupling_ref[n, c])
            blocks.append(jnp.where(half == even, raw, swap(raw)))
        blocks = jnp.where(lo192, jnp.concatenate(blocks, axis=0), 0.0)
        if n == 0:
            rows = blocks
        else:
            blocks = blocks.astype(BF16)
            high, low = carried[n]
            full = dot_t(blocks, jnp.concatenate([high, high], axis=0))
            if low is not None:
                full = full + dot_t(blocks, jnp.concatenate([low, low], axis=0))
            upper = full.astype(BF16).astype(F32)
            rows = jnp.where(lo192, upper, full - upper)
        coupled_ref[256 * n : 256 * n + 192, :] = rows.astype(BF16)
        coupled_ref[256 * n + 192 : 256 * n + 256, :] = jnp.zeros((64, 128), BF16)

    lo = low_half(16)
    nothing = jnp.zeros((16, 128), BF16)
    sub = lax.axis_index("sub")
    for d, ref in enumerate(sources):
        first = (sub ^ d) * 32
        for j in range(TILES):
            x = tile(ref, j)
            y = swap(x)
            for m, (a, b) in enumerate(((x, y), (y, x))):
                coeff_ref[0, first + 2 * j + m] = jnp.where(lo, a, nothing)
                coeff_ref[1, first + 2 * j + m] = jnp.where(lo, nothing, b)
    copies[5].wait()
    for leaf in range(32):
        for c in range(4):
            picked_ref[16 * leaf : 16 * leaf + 16, 128 * c : 128 * c + 128] = (
                coeff_ref[0, links_ref[2 * c, leaf] & 127]
                + coeff_ref[1, links_ref[2 * c + 1, leaf] & 127]
            )
    spread_ref[...] = dot(picked_ref[...], split).astype(BF16)
    for j in range(TILES):
        if j % 4 == 0:
            copies[6 + j // 4].wait()
        pair = []
        for leaf in (2 * j, 2 * j + 1):
            rows = spread_ref[16 * leaf : 16 * leaf + 16, :]
            pair.append(
                dot(jnp.concatenate([rows[:, :256], rows[:, 256:]], axis=0), coupling_ref[leaf])
            )
        a, b = pair
        linked_ref[:, 128 * j : 128 * j + 128] = jnp.where(
            lo, a[:16] + swap(a[16:]), swap(b[:16]) + b[16:]
        )


def downward_kernel(
    size_hbm, node_links_hbm, one_ref, three_ref, cross_ref, message_ref,
    linked_ref, field_ref, basis_ref, transfer_ref, nodes_ref, coupled_ref,
    out_ref,
    size_ref, node_links_ref, table_ref, sems,
):
    copies = start_all(sems, [(size_hbm, size_ref), (node_links_hbm, node_links_ref)])
    branch, sub = lax.axis_index("leaf"), lax.axis_index("sub")
    lo = low_half(16)
    lo8 = low_half(8)
    lo32 = low_half(32)

    pairs = []
    zeros = jnp.zeros((16, 128), BF16)
    for q in range(32):
        one, two = message_ref[2 * q].astype(F32), message_ref[2 * q + 1].astype(F32)
        one_s, two_s = swap(one), swap(two)
        pairs.append(
            jnp.concatenate([jnp.where(lo8, one, two_s), jnp.where(lo8, one_s, two)], axis=0).astype(BF16)
        )
        first = jnp.concatenate([jnp.where(lo8, one, one_s), jnp.where(lo8, one_s, one)], axis=0)
        second = jnp.concatenate([jnp.where(lo8, two, two_s), jnp.where(lo8, two_s, two)], axis=0)
        table_ref[64 + 2 * q] = jnp.concatenate([first.astype(BF16), zeros], axis=0)
        table_ref[65 + 2 * q] = jnp.concatenate([second.astype(BF16), zeros], axis=0)

    def weights(q):
        return nodes_ref[128 * (q - 8) : 128 * (q - 8) + 128, :]

    size = 32
    while size >= 8:
        parents = []
        for q in range(size, 2 * size):
            a = dot(pairs[q - size], weights(q))
            if size < 32:
                a = a[:16] + a[16:]
            high, low = pieces(a)
            parents.append(jnp.concatenate([high, low], axis=0))
            table_ref[q] = parents[-1]
        pairs = [jnp.where(lo32, parents[2 * q], parents[2 * q + 1]) for q in range(size // 2)]
        size = size // 2
    for copy in copies:
        copy.wait()
    sources = []
    for n in range(4):
        own = (64 >> n) + (branch >> n)
        a, b, c = [table_ref[node_links_ref[m, own]] for m in range(3)]
        sources += [jnp.where(lo32, a, b), c]
    down = dot(jnp.concatenate(sources, axis=1), coupled_ref[...])
    down = down[:16] + down[16:]
    down = (down + swap(down)).astype(BF16)
    half = low_half(64)
    blank = jnp.zeros((64, 128), BF16)

    def leaves(ref, j):
        both = ref[64 * j : 64 * j + 64, :]
        return jnp.concatenate([jnp.where(half, both, blank), jnp.where(half, blank, both)], axis=0)


    left = jnp.where(sub == 2, tile(three_ref, 18), tile(one_ref, 18))
    left = jnp.where(lo, zeros, jnp.where(sub == 0, cross_ref[...], left))
    right = jnp.where(sub == 1, tile(three_ref, 17), tile(one_ref, 17))
    right = jnp.where(lo, jnp.where(sub == 3, cross_ref[...], right), zeros)
    for j in range(TILES):
        far = (tile(linked_ref, j) + dot_t(down, leaves(transfer_ref, j))).astype(BF16)
        out = dot_t(far, leaves(basis_ref, j)) + tile(field_ref, j)
        if j == 0:
            out = out + dot_t(left, transfer_ref[1024:1152, :])
        if j == 15:
            out = out + dot_t(right, transfer_ref[1152:1280, :])
        out_ref[:, 128 * j : 128 * j + 128] = jnp.where(present(size_ref, j), out, 0.0).astype(BF16)


VMEM = pl.BlockSpec(memory_space=pltpu.VMEM)
HBM = pl.BlockSpec(memory_space=pltpu.HBM)


def shape(dims, dtype=BF16):
    return jax.ShapeDtypeStruct(dims, dtype)


def pinned(dims, dtype=BF16):
    return pltpu.VMEM(dims, dtype)


def stays(x):
    return pltpu.with_memory_space_constraint(x, pltpu.HBM)


def near_by(x):
    return pltpu.with_memory_space_constraint(x, pltpu.VMEM)


def call(kernel, name, outs, in_specs, out_specs, scratch, size, mib):
    return pl.pallas_call(
        kernel,
        out_shape=outs,
        in_specs=in_specs,
        out_specs=out_specs,
        scratch_shapes=scratch,
        compiler_params=pltpu.CompilerParams(vmem_limit_bytes=mib << 20),
        cost_estimate=pl.CostEstimate(flops=10**9, bytes_accessed=size, transcendentals=0),
        name=name,
    )


def dma(count):
    return pltpu.SemaphoreType.DMA((count,))


def upward(*args):
    return call(
        upward_kernel, "upward", [shape((16, PAYLOAD)), shape((16, 128))], [HBM] * 4, [VMEM] * 2,
        [
            pltpu.SMEM((32,), I32),
            pltpu.VMEM((16, 2048), BF16),
            pltpu.VMEM((4, 256, 128), BF16),
            pltpu.VMEM((4, 256, 128), BF16),
            pltpu.VMEM((16, 2048), BF16),
            pltpu.VMEM((512, 512), BF16),
            dma(4),
        ],
        10**6, 8,
    )(*args)


def near_field(*args):
    return call(
        near_kernel, "near",
        [
            pinned((16, 2048), F32), pinned((1024, 128)), pinned((1280, 128)), pinned((16, 128)),
        ],
        [HBM] * 5 + [VMEM], [VMEM] * 4,
        [
            pltpu.SMEM((32,), I32),
            pltpu.VMEM((16, 2048), BF16),
            pltpu.VMEM((3, 4, 256, 128), BF16),
            pltpu.VMEM((4, 256, 128), BF16),
            pltpu.VMEM((4, 256, 128), BF16),
            pltpu.VMEM((16, 18 * 128), BF16),
            pltpu.VMEM((6, 512, 128), F32),
            dma(5),
        ],
        3 * 10**6, 12,
    )(*args)


def message(*args):
    return call(
        message_kernel, "message", pinned((64, 8, 128)), [VMEM] * 4, VMEM, [], 10**5, 4
    )(*args)


def middle(*args):
    return call(
        middle_kernel, "middle",
        [pinned((56 * 128, 128)), pinned((1024, 128)), pinned((16, 2048), F32)],
        [HBM] * 4 + [VMEM] * 4, [VMEM] * 3,
        [
            pltpu.SMEM((8, 32), I32),
            pltpu.VMEM((14, 256, 128), BF16),
            pltpu.VMEM((4, 3, 256, 128), BF16),
            pltpu.VMEM((32, 256, 128), BF16),
            pltpu.VMEM((2, 512, 128), F32),
            pltpu.VMEM((2, 128, 16, 128), BF16),
            pltpu.VMEM((512, 512), BF16),
            pltpu.VMEM((512, 512), BF16),
            dma(10),
        ],
        6 * 10**6, 16,
    )(*args)


def downward(*args):
    return call(
        downward_kernel, "downward", shape((16, 2048)), [HBM] * 2 + [VMEM] * 10, VMEM,
        [
            pltpu.SMEM((32,), I32),
            pltpu.SMEM((3, 128), I32),
            pltpu.VMEM((128, 32, 128), BF16),
            dma(2),
        ],
        4 * 10**6, 8,
    )(*args)


def grouped(table):
    lead, rows = table.shape[:-2], table.shape[-2]
    table = jnp.swapaxes(table.reshape(*lead, rows // 8, 8, 32, 128), -3, -2)
    return table.reshape(*lead, rows // 8, 256, 128)


def body(
    vectors, leaf_size, leaf_basis, near_blocks, leaf_links, leaf_coupling, leaf_transfer,
    node_transfer, node_links, node_coupling,
):
    basis, transfer, nodes = grouped(leaf_basis), grouped(leaf_transfer), grouped(node_transfer)
    coupling = grouped(leaf_coupling)[:, 0]
    near = grouped(near_blocks.transpose(1, 0, 2))
    node_coupled = grouped(node_coupling.transpose(1, 0, 2))

    basis, transfer, nodes, coupling, near, node_coupled, vectors, leaf_size, links, node_links = map(
        stays,
        (
            basis, transfer, nodes, coupling, near, node_coupled, vectors, leaf_size, leaf_links.T,
            node_links.T,
        ),
    )
    payload, cross = upward(leaf_size, vectors, basis, transfer)
    others = [
        lax.ppermute(payload, "sub", [(s, s ^ d) for s in range(4)]) for d in (1, 2, 3)
    ]
    field, basis_p, transfer_p, share = near_field(
        leaf_size, vectors, near, basis, transfer, payload
    )

    messages = message(share, *others)
    summed = lax.all_to_all(messages, "leaf", 0, 0)

    branches = lax.axis_size("leaf")
    routes = [(4 * b + 3, 4 * b + 4) for b in range(branches - 1)]
    routes += [(4 * b, 4 * b - 1) for b in range(1, branches)]
    cross = lax.ppermute(cross, ("leaf", "sub"), routes)

    nodes_p, coupled, linked = middle(
        nodes, node_coupled, links, coupling, payload, *others
    )
    return downward(
        leaf_size, node_links, others[0], others[2], cross, summed,
        *map(near_by, (linked, field, basis_p, transfer_p, nodes_p, coupled)),
    )


def solution(mesh):
    split = ("leaf", "sub")
    placed = (
        P(None, split), P(split), P(split, None), P(split, None, None), P(split, None),
        P(split, None, None), P(split, None), P(), P(), P(),
    )
    return jax.shard_map(
        body, mesh=mesh, in_specs=placed, out_specs=P(None, split), check_vma=False
    )
```

```python
import jax
import jax.numpy as jnp
from jax import lax
from jax.experimental import pallas as pl
from jax.experimental.pallas import tpu as pltpu
from jax.sharding import PartitionSpec as P

F32, BF16, I32 = jnp.float32, jnp.bfloat16, jnp.int32
TILES = 16
COEFF = 16 * 128
PAYLOAD = 19 * 128


def iota(shape, dim):
    return lax.broadcasted_iota(I32, shape, dim)


def dot(a, b):
    return jnp.dot(a, b, preferred_element_type=F32)


def dot_t(a, b):
    return lax.dot_general(a, b, (((1,), (1,)), ((), ())), preferred_element_type=F32)


def swap(x):
    return pltpu.roll(x, 64, 1)


def low_half(rows):
    return iota((rows, 128), 1) < 64


def tile(ref, j):
    return ref[:, 128 * j : 128 * j + 128]


def pieces(x):
    high = x.astype(BF16)
    return high, (x - high.astype(F32)).astype(BF16)


def split_map():
    row = iota((512, 128), 0)
    rank = row & 63
    target = (rank & 1) * 256 + (rank >> 1) * 8 + (row >> 6) - iota((512, 128), 1)
    return jnp.concatenate(
        [jnp.where(target == 128 * q, 1.0, 0.0).astype(BF16) for q in range(4)], axis=1
    )


def group_map():
    row, col = iota((256, 256), 0), iota((256, 256), 1)
    return jnp.where(col == (row & 31) * 8 + (row >> 5), 1.0, 0.0).astype(BF16)


def plain_rows(raw, rows_ref):
    count = raw.shape[0]
    lo = low_half(count)
    other = swap(raw)
    rows_ref[pl.ds(0, count, stride=2), :] = jnp.where(lo, raw, other)
    rows_ref[pl.ds(1, count, stride=2), :] = jnp.where(lo, other, raw)


def present(size_ref, j):
    lane = iota((16, 128), 1)
    limit = jnp.where(lane < 64, size_ref[2 * j], size_ref[2 * j + 1])
    return (lane & 63) < limit


def kept(size_ref, x_ref, j):
    return jnp.where(present(size_ref, j), tile(x_ref, j).astype(F32), 0.0)


def start_all(sems, pairs):
    copies = [pltpu.make_async_copy(a, b, sems.at[n]) for n, (a, b) in enumerate(pairs)]
    for copy in copies:
        copy.start()
    return copies


def upward_kernel(
    size_hbm, x_hbm, basis_hbm, transfer_hbm, pay_ref,
    size_ref, x_ref, basis_ref, transfer_ref, masked_ref, map_ref, sems,
):
    copies = start_all(
        sems,
        [(x_hbm, x_ref), (size_hbm, size_ref), (basis_hbm, basis_ref), (transfer_hbm, transfer_ref)],
    )
    lo = low_half(16)
    map_ref[...] = split_map()
    copies[0].wait()
    copies[1].wait()
    for j in range(TILES):
        masked_ref[:, 128 * j : 128 * j + 128] = kept(size_ref, x_ref, j).astype(BF16)
    points = jnp.concatenate([masked_ref[:, 512 * g : 512 * g + 512] for g in range(4)], axis=0)
    spread = dot(points, map_ref[...]).astype(BF16)
    member = iota((16, 256), 1) & 7
    picks = [jnp.where(member == m, 1.0, 0.0).astype(BF16) for m in range(8)]
    copies[2].wait()
    for g in range(4):
        halves = [spread[16 * g : 16 * g + 16, 256 * h : 256 * h + 256] for h in range(2)]
        rows = jnp.concatenate([halves[h] * picks[m] for m in range(8) for h in range(2)], axis=0)
        out = dot(rows, basis_ref[g])
        for q in range(4):
            a0, a1, b0, b1 = [out[64 * q + 16 * n : 64 * q + 16 * n + 16] for n in range(4)]
            coeff = jnp.where(lo, a0 + swap(a1), swap(b0) + b1)
            j = 4 * g + q
            pay_ref[:, 128 * j : 128 * j + 128] = coeff.astype(BF16)
    coeffs = jnp.concatenate([pay_ref[:, 512 * g : 512 * g + 512] for g in range(4)], axis=0)
    spread = dot(coeffs, map_ref[...]).astype(BF16)
    copies[3].wait()
    total = jnp.zeros((32, 128), F32)
    for g in range(4):
        rows = jnp.concatenate(
            [spread[16 * g : 16 * g + 16, 256 * h : 256 * h + 256] for h in range(2)], axis=0
        )
        total = total + dot(rows, transfer_ref[g])
    share = jnp.where(lo, total[:16] + swap(total[16:]), swap(total[:16]) + total[16:])
    packed = jnp.where(low_half(8), share[:8], share[8:])
    high = packed.astype(BF16).astype(F32)
    pay_ref[:, COEFF : COEFF + 128] = jnp.concatenate([high, packed - high], axis=0).astype(BF16)
    pay_ref[:, COEFF + 128 : COEFF + 256] = tile(masked_ref, 0)
    pay_ref[:, COEFF + 256 : COEFF + 384] = tile(masked_ref, 15)


def near_kernel(
    size_hbm, x_hbm, near_hbm, basis_hbm, transfer_hbm, pay_ref,
    field_ref, basis_rows, carry_rows, share_ref,
    size_ref, x_ref, near_ref, basis_ref, transfer_ref, masked_ref, raw_ref, sems,
):
    copies = start_all(
        sems,
        [
            (basis_hbm, basis_ref), (transfer_hbm, transfer_ref), (x_hbm, x_ref), (size_hbm, size_ref),
            (near_hbm, near_ref),
        ],
    )
    share_ref[...] = tile(pay_ref, 16)
    collect = group_map()
    half = low_half(64)
    row = iota((64, 128), 0)
    for copy in copies:
        copy.wait()
    for g in range(4):
        raw = dot(collect, jnp.concatenate([basis_ref[g], transfer_ref[g]], axis=1))
        for n in range(2):
            plain_rows(raw[:, 128 * n : 128 * n + 128], raw_ref.at[2 * g + n])
        for q in range(4):
            j = 4 * g + q
            pair = [raw_ref[2 * g, 128 * q + 64 * m : 128 * q + 64 * m + 64, :] for m in range(2)]
            pair = [jnp.where(row < size_ref[2 * j + m], pair[m], 0.0) for m in range(2)]
            start = 64 * j
            basis_rows[start : start + 64, :] = jnp.where(half, *pair).astype(BF16)
            blocks = jnp.concatenate([jnp.where(half, pair[0], 0.0), jnp.where(half, 0.0, pair[1])], axis=0)
            carry = dot(blocks.astype(BF16), raw_ref[2 * g + 1, 128 * q : 128 * q + 128, :].astype(BF16))
            carry_rows[start : start + 64, :] = jnp.where(half, carry[:64], carry[64:]).astype(BF16)
    masked_ref[:, 0:128] = jnp.zeros((16, 128), BF16)
    masked_ref[:, 17 * 128 : 18 * 128] = jnp.zeros((16, 128), BF16)
    for j in range(TILES):
        masked_ref[:, 128 * j + 128 : 128 * j + 256] = kept(size_ref, x_ref, j).astype(BF16)
    lo = low_half(16)
    for pair in range(2):
        for s in range(3):
            raw = dot(
                collect, jnp.concatenate([near_ref[s, 2 * pair], near_ref[s, 2 * pair + 1]], axis=1)
            )
            for n in range(2):
                plain_rows(raw[:, 128 * n : 128 * n + 128], raw_ref.at[3 * n + s])
        for q in range(8):
            j = 8 * pair + q
            at = 128 * (q % 4)
            a = [raw_ref[3 * (q // 4) + s, at : at + 64, :] for s in range(3)]
            b = [raw_ref[3 * (q // 4) + s, at + 64 : at + 128, :] for s in range(3)]
            inner = jnp.concatenate([jnp.where(half, a[1], a[2]), jnp.where(half, b[0], b[1])], axis=0)
            outer = jnp.concatenate([jnp.where(half, 0.0, a[0]), jnp.where(half, b[2], 0.0)], axis=0)
            if j in (0, 15):
                start = 1024 + 128 * (j // 15)
                limit = jnp.where(iota((128, 128), 0) < 64, size_ref[2 * j], size_ref[2 * j + 1])
                edge = jnp.where((iota((128, 128), 0) & 63) < limit, outer, 0.0)
                carry_rows[start : start + 128, :] = edge.astype(BF16)
            outer = outer.astype(BF16)
            around = jnp.where(lo, tile(masked_ref, j + 2), tile(masked_ref, j))
            near = dot_t(
                jnp.concatenate([tile(masked_ref, j + 1), around], axis=1),
                jnp.concatenate([inner.astype(BF16), outer], axis=1),
            )
            field_ref[:, 128 * j : 128 * j + 128] = jnp.where(present(size_ref, j), near, 0.0)


def message_kernel(share_ref, one_ref, two_ref, three_ref, out_ref, cross_ref, sides_ref):
    total = share_ref[...].astype(F32)
    for ref in (one_ref, two_ref, three_ref):
        total = total + tile(ref, 16).astype(F32)
    packed = (total[:8] + total[8:]).astype(BF16)
    for n in range(64):
        out_ref[n] = packed
    sub = lax.axis_index("sub")
    cross_ref[...] = jnp.where(sub == 0, tile(three_ref, 18), tile(three_ref, 17))
    sides_ref[0] = jnp.where(sub == 2, tile(three_ref, 18), tile(one_ref, 18))
    sides_ref[1] = jnp.where(sub == 1, tile(three_ref, 17), tile(one_ref, 17))


def middle_kernel(
    nodes_hbm, node_coupling_hbm, links_hbm, node_links_hbm, coupling_hbm,
    own_ref, two_ref, three_ref, one_ref, near_ref, basis_ref,
    rows_ref, coupled_ref, field_ref, node_links_ref,
    links_ref, nodes_ref, node_coupling_ref, coupling_ref,
    raw_ref, coeff_ref, picked_ref, spread_ref, sems,
):
    branch = lax.axis_index("leaf")
    own = [64 + branch, 32 + (branch >> 1), 16 + (branch >> 2), 8 + (branch >> 3)]
    sources = (own_ref, one_ref, two_ref, three_ref)
    copies = start_all(
        sems,
        [(nodes_hbm.at[pl.ds(2, 14)], nodes_ref)]
        + [(node_coupling_hbm.at[:, own[n] >> 3], node_coupling_ref.at[n]) for n in range(4)]
        + [(links_hbm, links_ref)]
        + [(coupling_hbm.at[pl.ds(8 * n, 8)], coupling_ref.at[pl.ds(8 * n, 8)]) for n in range(4)]
        + [(node_links_hbm, node_links_ref)],
    )
    collect = group_map()
    split = split_map()
    lo = low_half(16)
    nothing = jnp.zeros((16, 128), BF16)
    half = low_half(64)
    blank = jnp.zeros((64, 128), BF16)
    sub = lax.axis_index("sub")
    for d, ref in enumerate(sources):
        first = (sub ^ d) * 32
        for j in range(TILES):
            x = tile(ref, j)
            y = swap(x)
            for m, (a, b) in enumerate(((x, y), (y, x))):
                coeff_ref[0, first + 2 * j + m] = jnp.where(lo, a, nothing)
                coeff_ref[1, first + 2 * j + m] = jnp.where(lo, nothing, b)
    copies[5].wait()
    for leaf in range(32):
        for c in range(4):
            picked_ref[16 * leaf : 16 * leaf + 16, 128 * c : 128 * c + 128] = (
                coeff_ref[0, links_ref[2 * c, leaf] & 127]
                + coeff_ref[1, links_ref[2 * c + 1, leaf] & 127]
            )
    spread_ref[...] = dot(picked_ref[...], split).astype(BF16)
    for copy in copies[:5] + copies[6:]:
        copy.wait()
    for g in range(0, 14, 2):
        raw = dot(collect, jnp.concatenate([nodes_ref[g], nodes_ref[g + 1]], axis=1))
        for n in range(2):
            plain_rows(raw[:, 128 * n : 128 * n + 128], raw_ref.at[n])
            rows_ref[512 * (g + n) : 512 * (g + n) + 512, :] = raw_ref[n].astype(BF16)

    half = low_half(64)
    row, col = iota((64, 256), 0), iota((64, 256), 1)
    even = (iota((64, 128), 0) & 1) == 0

    def node(n):
        return rows_ref[pl.ds(pl.multiple_of((own[n] - 16) * 64, 64), 64), :]

    carried = [None, (node(0), None)]
    for n in (1, 2):
        high, low = carried[n]
        longer = dot(high[:, :64], node(n))
        if low is not None:
            longer = longer + dot(low[:, :64], node(n))
        carried.append(pieces(longer))
    lo192 = low_half(192)
    for n in range(4):
        pick = jnp.where(((row >> 1) == (col >> 3)) & ((col & 7) == (own[n] & 7)), 1.0, 0.0).astype(BF16)
        blocks = []
        for c in range(3):
            raw = dot(pick, node_coupling_ref[n, c])
            blocks.append(jnp.where(half == even, raw, swap(raw)))
        blocks = jnp.where(lo192, jnp.concatenate(blocks, axis=0), 0.0)
        if n == 0:
            rows = blocks
        else:
            blocks = blocks.astype(BF16)
            high, low = carried[n]
            full = dot_t(blocks, jnp.concatenate([high, high], axis=0))
            if low is not None:
                full = full + dot_t(blocks, jnp.concatenate([low, low], axis=0))
            upper = full.astype(BF16).astype(F32)
            rows = jnp.where(lo192, upper, full - upper)
        coupled_ref[256 * n : 256 * n + 192, :] = rows.astype(BF16)
        coupled_ref[256 * n + 192 : 256 * n + 256, :] = jnp.zeros((64, 128), BF16)

    for j in range(TILES):
        rows = spread_ref[32 * j : 32 * j + 32, :]
        both = dot(
            jnp.concatenate([rows[:, :256], rows[:, 256:]], axis=0),
            jnp.concatenate([coupling_ref[2 * j], coupling_ref[2 * j + 1]], axis=1),
        )
        a = jnp.concatenate([both[:16, :128], both[32:48, :128]], axis=0)
        b = jnp.concatenate([both[16:32, 128:], both[48:, 128:]], axis=0)
        far = jnp.where(lo, a[:16] + swap(a[16:]), swap(b[:16]) + b[16:]).astype(BF16)
        rows = basis_ref[64 * j : 64 * j + 64, :]
        blocks = jnp.concatenate([jnp.where(half, rows, blank), jnp.where(half, blank, rows)], axis=0)
        field_ref[:, 128 * j : 128 * j + 128] = tile(near_ref, j) + dot_t(far, blocks)


def downward_kernel(
    links_ref, sides_ref, cross_ref, message_ref,
    field_ref, carry_ref, nodes_ref, coupled_ref,
    out_ref,
    node_links_ref, table_ref, sem,
):
    copy = pltpu.make_async_copy(links_ref, node_links_ref, sem)
    copy.start()
    branch, sub = lax.axis_index("leaf"), lax.axis_index("sub")
    lo = low_half(16)
    lo8 = low_half(8)
    lo32 = low_half(32)

    zeros = jnp.zeros((16, 128), BF16)

    def weights(k):
        return nodes_ref[pl.ds(pl.multiple_of(128 * (k - 8), 128), 128), :]

    for q in range(32):
        one, two = message_ref[2 * q].astype(F32), message_ref[2 * q + 1].astype(F32)
        pair = jnp.concatenate(
            [jnp.where(lo8, one, swap(two)), jnp.where(lo8, swap(one), two)], axis=0
        )
        value = dot(pair.astype(BF16), nodes_ref[128 * (q + 24) : 128 * (q + 24) + 128, :])
        table_ref[q] = jnp.concatenate(pieces(value), axis=0)

    def leaf_node(k):
        one = message_ref[k - 64].astype(F32)
        other = swap(one)
        rows = jnp.concatenate([jnp.where(lo8, one, other), jnp.where(lo8, other, one)], axis=0)
        return jnp.concatenate([rows.astype(BF16), zeros], axis=0)

    def parent(k, children):
        value = dot(jnp.where(lo32, *children), weights(k))
        return jnp.concatenate(pieces(value[:16] + value[16:]), axis=0)

    copy.wait()
    ends = [[node_links_ref[m, (64 >> n) + (branch >> n)] for m in range(3)] for n in range(4)]
    sixteen = ends[2] + [2 * k + m for k in ends[3] for m in range(2)]
    values = [parent(k, [table_ref[2 * k - 32], table_ref[2 * k - 31]]) for k in sixteen]
    found = [
        [leaf_node(k) for k in ends[0]],
        [table_ref[k - 32] for k in ends[1]],
        values[:3],
        [parent(k, values[3 + 2 * n : 5 + 2 * n]) for n, k in enumerate(ends[3])],
    ]
    sources = []
    for a, b, c in found:
        sources += [jnp.where(lo32, a, b), c]
    down = dot(jnp.concatenate(sources, axis=1), coupled_ref[...])
    down = down[:16] + down[16:]
    down = (down + swap(down)).astype(BF16)
    ends = jnp.concatenate([jnp.where(lo, down, zeros), jnp.where(lo, zeros, down)], axis=0)
    shared = dot_t(ends, carry_ref[0:1024, :])
    left = jnp.where(lo, zeros, jnp.where(sub == 0, cross_ref[...], sides_ref[0]))
    right = jnp.where(lo, jnp.where(sub == 3, cross_ref[...], sides_ref[1]), zeros)
    for t in range(8):
        a, b = shared[:16, 128 * t : 128 * t + 128], shared[16:, 128 * t : 128 * t + 128]
        for j, far in ((2 * t, jnp.where(lo, a, swap(b))), (2 * t + 1, jnp.where(lo, swap(a), b))):
            out = far + tile(field_ref, j)
            if j == 0:
                out = out + dot_t(left, carry_ref[1024:1152, :])
            if j == 15:
                out = out + dot_t(right, carry_ref[1152:1280, :])
            out_ref[:, 128 * j : 128 * j + 128] = out.astype(BF16)


VMEM = pl.BlockSpec(memory_space=pltpu.VMEM)
HBM = pl.BlockSpec(memory_space=pltpu.HBM)


def shape(dims, dtype=BF16):
    return jax.ShapeDtypeStruct(dims, dtype)


def pinned(dims, dtype=BF16):
    return pltpu.VMEM(dims, dtype)


def stays(x):
    return pltpu.with_memory_space_constraint(x, pltpu.HBM)


def near_by(x):
    return pltpu.with_memory_space_constraint(x, pltpu.VMEM)


def call(kernel, name, outs, in_specs, out_specs, scratch, size, mib):
    return pl.pallas_call(
        kernel,
        out_shape=outs,
        in_specs=in_specs,
        out_specs=out_specs,
        scratch_shapes=scratch,
        compiler_params=pltpu.CompilerParams(vmem_limit_bytes=mib << 20),
        cost_estimate=pl.CostEstimate(flops=10**9, bytes_accessed=size, transcendentals=0),
        name=name,
    )


def dma(count):
    return pltpu.SemaphoreType.DMA((count,))


def upward(*args):
    return call(
        upward_kernel, "upward", shape((16, PAYLOAD)), [HBM] * 4, VMEM,
        [
            pltpu.SMEM((32,), I32),
            pltpu.VMEM((16, 2048), BF16),
            pltpu.VMEM((4, 256, 128), BF16),
            pltpu.VMEM((4, 256, 128), BF16),
            pltpu.VMEM((16, 2048), BF16),
            pltpu.VMEM((512, 512), BF16),
            dma(4),
        ],
        10**6, 8,
    )(*args)


def near_field(*args):
    return call(
        near_kernel, "near",
        [
            pinned((16, 2048), F32), pinned((1024, 128)), pinned((1280, 128)), pinned((16, 128)),
        ],
        [HBM] * 5 + [VMEM], [VMEM] * 4,
        [
            pltpu.SMEM((32,), I32),
            pltpu.VMEM((16, 2048), BF16),
            pltpu.VMEM((3, 4, 256, 128), BF16),
            pltpu.VMEM((4, 256, 128), BF16),
            pltpu.VMEM((4, 256, 128), BF16),
            pltpu.VMEM((16, 18 * 128), BF16),
            pltpu.VMEM((8, 512, 128), F32),
            dma(5),
        ],
        3 * 10**6, 12,
    )(*args)


def message(*args):
    return call(
        message_kernel, "message", [shape((64, 8, 128)), shape((16, 128)), shape((2, 16, 128))], [VMEM] * 4, [VMEM] * 3, [],
        10**5, 4,
    )(*args)


def middle(*args):
    return call(
        middle_kernel, "middle",
        [pinned((56 * 128, 128)), pinned((1024, 128)), pinned((16, 2048), F32), pinned((3, 128), I32)],
        [HBM] * 5 + [VMEM] * 6, [VMEM] * 4,
        [
            pltpu.SMEM((8, 32), I32),
            pltpu.VMEM((14, 256, 128), BF16),
            pltpu.VMEM((4, 3, 256, 128), BF16),
            pltpu.VMEM((32, 256, 128), BF16),
            pltpu.VMEM((2, 512, 128), F32),
            pltpu.VMEM((2, 128, 16, 128), BF16),
            pltpu.VMEM((512, 512), BF16),
            pltpu.VMEM((512, 512), BF16),
            dma(11),
        ],
        6 * 10**6, 16,
    )(*args)


def downward(*args):
    return call(
        downward_kernel, "downward", shape((16, 2048)), [VMEM] * 8, VMEM,
        [pltpu.SMEM((3, 128), I32), pltpu.VMEM((32, 32, 128), BF16), pltpu.SemaphoreType.DMA],
        4 * 10**6, 8,
    )(*args)


def grouped(table):
    lead, rows = table.shape[:-2], table.shape[-2]
    table = jnp.swapaxes(table.reshape(*lead, rows // 8, 8, 32, 128), -3, -2)
    return table.reshape(*lead, rows // 8, 256, 128)


def body(
    vectors, leaf_size, leaf_basis, near_blocks, leaf_links, leaf_coupling, leaf_transfer,
    node_transfer, node_links, node_coupling,
):
    basis, transfer, nodes = grouped(leaf_basis), grouped(leaf_transfer), grouped(node_transfer)
    coupling = grouped(leaf_coupling)[:, 0]
    near = grouped(near_blocks.transpose(1, 0, 2))
    node_coupled = grouped(node_coupling.transpose(1, 0, 2))

    basis, transfer, nodes, coupling, near, node_coupled, vectors, leaf_size, links, node_links = map(
        stays,
        (
            basis, transfer, nodes, coupling, near, node_coupled, vectors, leaf_size, leaf_links.T,
            node_links.T,
        ),
    )
    payload = upward(leaf_size, vectors, basis, transfer)
    others = [
        lax.ppermute(payload, "sub", [(s, s ^ d) for s in range(4)]) for d in (1, 2, 3)
    ]
    near_part, basis_p, carry, share = near_field(
        leaf_size, vectors, near, basis, transfer, payload
    )

    messages, cross, sides = message(share, *others)
    summed = lax.all_to_all(messages, "leaf", 0, 0)

    branches = lax.axis_size("leaf")
    routes = [(4 * b, 4 * b + 4) for b in range(branches - 1)]
    routes += [(4 * b + 3, 4 * b - 1) for b in range(1, branches)]
    cross = lax.ppermute(cross, ("leaf", "sub"), routes)

    nodes_p, coupled, field, partners = middle(
        nodes, node_coupled, links, node_links, coupling, payload, others[1], others[2], others[0],
        near_by(near_part), near_by(basis_p),
    )
    return downward(
        near_by(partners), sides, cross, summed,
        *map(near_by, (field, carry, nodes_p, coupled)),
    )


def solution(mesh):
    split = ("leaf", "sub")
    placed = (
        P(None, split), P(split), P(split, None), P(split, None, None), P(split, None),
        P(split, None, None), P(split, None), P(), P(), P(),
    )
    return jax.shard_map(
        body, mesh=mesh, in_specs=placed, out_specs=P(None, split), check_vma=False
    )
```

```python
import jax
import jax.numpy as jnp
from jax import lax
from jax.experimental import pallas as pl
from jax.experimental.pallas import tpu as pltpu
from jax.sharding import PartitionSpec as P

F32, BF16, I32 = jnp.float32, jnp.bfloat16, jnp.int32
TILES = 16
COEFF = 16 * 128
PAYLOAD = 19 * 128


def iota(shape, dim):
    return lax.broadcasted_iota(I32, shape, dim)


def dot(a, b):
    return jnp.dot(a, b, preferred_element_type=F32)


def dot_t(a, b):
    return lax.dot_general(a, b, (((1,), (1,)), ((), ())), preferred_element_type=F32)


def swap(x):
    return pltpu.roll(x, 64, 1)


def low_half(rows):
    return iota((rows, 128), 1) < 64


def tile(ref, j):
    return ref[:, 128 * j : 128 * j + 128]


def pieces(x):
    high = x.astype(BF16)
    return high, (x - high.astype(F32)).astype(BF16)


def split_map():
    row = iota((512, 128), 0)
    rank = row & 63
    target = (rank & 1) * 256 + (rank >> 1) * 8 + (row >> 6) - iota((512, 128), 1)
    return jnp.concatenate(
        [jnp.where(target == 128 * q, 1.0, 0.0).astype(BF16) for q in range(4)], axis=1
    )


def group_map():
    row, col = iota((256, 256), 0), iota((256, 256), 1)
    return jnp.where(col == (row & 31) * 8 + (row >> 5), 1.0, 0.0).astype(BF16)


def plain_rows(raw, rows_ref):
    count = raw.shape[0]
    lo = low_half(count)
    other = swap(raw)
    rows_ref[pl.ds(0, count, stride=2), :] = jnp.where(lo, raw, other)
    rows_ref[pl.ds(1, count, stride=2), :] = jnp.where(lo, other, raw)


def present(size_ref, j):
    lane = iota((16, 128), 1)
    limit = jnp.where(lane < 64, size_ref[2 * j], size_ref[2 * j + 1])
    return (lane & 63) < limit


def kept(size_ref, x_ref, j):
    return jnp.where(present(size_ref, j), tile(x_ref, j).astype(F32), 0.0)


def start_all(sems, pairs):
    copies = [pltpu.make_async_copy(a, b, sems.at[n]) for n, (a, b) in enumerate(pairs)]
    for copy in copies:
        copy.start()
    return copies


def upward_kernel(
    size_hbm, x_hbm, basis_hbm, transfer_hbm, near_hbm, nodes_hbm, links_hbm,
    pay_ref, masked_ref, limits_ref, basis_ref, transfer_ref, near_ref, nodes_ref, links_ref,
    size_ref, x_ref, map_ref, sems,
):
    copies = start_all(
        sems,
        [
            (x_hbm, x_ref), (size_hbm, size_ref), (basis_hbm, basis_ref), (transfer_hbm, transfer_ref),
            (near_hbm, near_ref), (nodes_hbm.at[pl.ds(2, 14)], nodes_ref), (links_hbm, links_ref),
        ],
    )
    lo = low_half(16)
    map_ref[...] = split_map()
    copies[0].wait()
    copies[1].wait()
    for j in range(TILES):
        masked_ref[:, 128 * j : 128 * j + 128] = kept(size_ref, x_ref, j).astype(BF16)
    points = jnp.concatenate([masked_ref[:, 512 * g : 512 * g + 512] for g in range(4)], axis=0)
    spread = dot(points, map_ref[...]).astype(BF16)
    member = iota((16, 256), 1) & 7
    picks = [jnp.where(member == m, 1.0, 0.0).astype(BF16) for m in range(8)]
    copies[2].wait()
    for g in range(4):
        halves = [spread[16 * g : 16 * g + 16, 256 * h : 256 * h + 256] for h in range(2)]
        rows = jnp.concatenate([halves[h] * picks[m] for m in range(8) for h in range(2)], axis=0)
        out = dot(rows, basis_ref[g])
        for q in range(4):
            a0, a1, b0, b1 = [out[64 * q + 16 * n : 64 * q + 16 * n + 16] for n in range(4)]
            coeff = jnp.where(lo, a0 + swap(a1), swap(b0) + b1)
            j = 4 * g + q
            pay_ref[:, 128 * j : 128 * j + 128] = coeff.astype(BF16)
    coeffs = jnp.concatenate([pay_ref[:, 512 * g : 512 * g + 512] for g in range(4)], axis=0)
    spread = dot(coeffs, map_ref[...]).astype(BF16)
    copies[3].wait()
    total = jnp.zeros((32, 128), F32)
    for g in range(4):
        rows = jnp.concatenate(
            [spread[16 * g : 16 * g + 16, 256 * h : 256 * h + 256] for h in range(2)], axis=0
        )
        total = total + dot(rows, transfer_ref[g])
    share = jnp.where(lo, total[:16] + swap(total[16:]), swap(total[:16]) + total[16:])
    packed = jnp.where(low_half(8), share[:8], share[8:])
    high = packed.astype(BF16).astype(F32)
    pay_ref[:, COEFF : COEFF + 128] = jnp.concatenate([high, packed - high], axis=0).astype(BF16)
    pay_ref[:, COEFF + 128 : COEFF + 256] = tile(masked_ref, 0)
    pay_ref[:, COEFF + 256 : COEFF + 384] = tile(masked_ref, 15)
    for n in range(32):
        limits_ref[n : n + 1, :] = jnp.full((1, 128), size_ref[n], I32)
    for copy in copies[4:]:
        copy.wait()


def near_kernel(
    kept_ref, limits_ref, near_ref, basis_ref, transfer_ref, nodes_ref, pay_ref,
    field_ref, basis_rows, carry_rows, edge_ref, share_ref, node_rows,
    masked_ref, raw_ref, node_raw,
):
    share_ref[...] = tile(pay_ref, 16)
    lane = iota((16, 128), 1)
    collect = group_map()
    half = low_half(64)
    row = iota((64, 128), 0)
    for g in range(4):
        raw = dot(collect, jnp.concatenate([basis_ref[g], transfer_ref[g]], axis=1))
        for n in range(2):
            plain_rows(raw[:, 128 * n : 128 * n + 128], raw_ref.at[2 * g + n])
        for q in range(4):
            j = 4 * g + q
            pair = [raw_ref[2 * g, 128 * q + 64 * m : 128 * q + 64 * m + 64, :] for m in range(2)]
            pair = [jnp.where(row < limits_ref[2 * j + m : 2 * j + m + 1, :], pair[m], 0.0) for m in range(2)]
            start = 64 * j
            basis_rows[start : start + 64, :] = jnp.where(half, *pair).astype(BF16)
            blocks = jnp.concatenate([jnp.where(half, pair[0], 0.0), jnp.where(half, 0.0, pair[1])], axis=0)
            carry = dot(blocks.astype(BF16), raw_ref[2 * g + 1, 128 * q : 128 * q + 128, :].astype(BF16))
            carry_rows[start : start + 64, :] = jnp.where(half, carry[:64], carry[64:]).astype(BF16)
    masked_ref[:, 0:128] = jnp.zeros((16, 128), BF16)
    masked_ref[:, 17 * 128 : 18 * 128] = jnp.zeros((16, 128), BF16)
    masked_ref[:, 128 : 17 * 128] = kept_ref[...]
    lo = low_half(16)
    for pair in range(2):
        for s in range(3):
            raw = dot(
                collect, jnp.concatenate([near_ref[s, 2 * pair], near_ref[s, 2 * pair + 1]], axis=1)
            )
            for n in range(2):
                plain_rows(raw[:, 128 * n : 128 * n + 128], raw_ref.at[3 * n + s])
        for q in range(8):
            j = 8 * pair + q
            at = 128 * (q % 4)
            a = [raw_ref[3 * (q // 4) + s, at : at + 64, :] for s in range(3)]
            b = [raw_ref[3 * (q // 4) + s, at + 64 : at + 128, :] for s in range(3)]
            inner = jnp.concatenate([jnp.where(half, a[1], a[2]), jnp.where(half, b[0], b[1])], axis=0)
            outer = jnp.concatenate([jnp.where(half, 0.0, a[0]), jnp.where(half, b[2], 0.0)], axis=0)
            if j in (0, 15):
                edge = jnp.concatenate(
                    [
                        jnp.where(row < limits_ref[2 * j + m : 2 * j + m + 1, :], outer[64 * m : 64 * m + 64], 0.0)
                        for m in range(2)
                    ],
                    axis=0,
                )
                edge_ref[j // 15] = edge.astype(BF16)
            outer = outer.astype(BF16)
            around = jnp.where(lo, tile(masked_ref, j + 2), tile(masked_ref, j))
            near = dot_t(
                jnp.concatenate([tile(masked_ref, j + 1), around], axis=1),
                jnp.concatenate([inner.astype(BF16), outer], axis=1),
            )
            field_ref[:, 128 * j : 128 * j + 128] = jnp.where(
                (lane & 63) < jnp.where(lane < 64, limits_ref[2 * j : 2 * j + 1, :], limits_ref[2 * j + 1 : 2 * j + 2, :]),
                near,
                0.0,
            )
    for g in range(0, 14, 2):
        raw = dot(collect, jnp.concatenate([nodes_ref[g], nodes_ref[g + 1]], axis=1))
        for n in range(2):
            plain_rows(raw[:, 128 * n : 128 * n + 128], node_raw.at[(g + n) % 4])
            node_rows[512 * (g + n) : 512 * (g + n) + 512, :] = node_raw[(g + n) % 4].astype(BF16)


def message_kernel(share_ref, one_ref, two_ref, three_ref, out_ref, cross_ref, sides_ref):
    total = share_ref[...].astype(F32)
    for ref in (one_ref, two_ref, three_ref):
        total = total + tile(ref, 16).astype(F32)
    packed = (total[:8] + total[8:]).astype(BF16)
    for n in range(64):
        out_ref[n] = packed
    sub = lax.axis_index("sub")
    cross_ref[...] = jnp.where(sub == 0, tile(three_ref, 18), tile(three_ref, 17))
    sides_ref[0] = jnp.where(sub == 2, tile(three_ref, 18), tile(one_ref, 18))
    sides_ref[1] = jnp.where(sub == 1, tile(three_ref, 17), tile(one_ref, 17))


def middle_kernel(
    node_coupling_hbm, links_vmem, node_links_hbm, coupling_hbm, rows_ref,
    own_ref, two_ref, three_ref, one_ref, near_ref, basis_ref, carry_rows,
    coupled_ref, field_ref, carry_ref, node_links_ref,
    links_ref, node_coupling_ref, coupling_ref, coeff_ref, picked_ref, spread_ref, sems,
):
    branch = lax.axis_index("leaf")
    own = [64 + branch, 32 + (branch >> 1), 16 + (branch >> 2), 8 + (branch >> 3)]
    sources = (own_ref, one_ref, two_ref, three_ref)
    copies = start_all(
        sems,
        [(links_vmem, links_ref)]
        + [(coupling_hbm.at[pl.ds(8 * n, 8)], coupling_ref.at[pl.ds(8 * n, 8)]) for n in range(4)]
        + [(node_coupling_hbm.at[:, own[n] >> 3], node_coupling_ref.at[n]) for n in range(4)]
        + [(node_links_hbm, node_links_ref)],
    )
    split = split_map()
    unit = jnp.where(iota((128, 128), 0) == iota((128, 128), 1), 1.0, 0.0).astype(BF16)
    for j in range(TILES):
        rows = carry_rows[64 * j : 64 * j + 64, :]
        turned = dot_t(unit, jnp.concatenate([rows, rows], axis=0))
        carry_ref[:, 128 * j : 128 * j + 128] = jnp.where(low_half(64), turned[:64], turned[64:]).astype(BF16)
    lo = low_half(16)
    nothing = jnp.zeros((16, 128), BF16)
    half = low_half(64)
    blank = jnp.zeros((64, 128), BF16)
    sub = lax.axis_index("sub")
    for d, ref in enumerate(sources):
        first = (sub ^ d) * 32
        for j in range(TILES):
            x = tile(ref, j)
            y = swap(x)
            for m, (a, b) in enumerate(((x, y), (y, x))):
                coeff_ref[0, first + 2 * j + m] = jnp.where(lo, a, nothing)
                coeff_ref[1, first + 2 * j + m] = jnp.where(lo, nothing, b)
    copies[0].wait()
    for leaf in range(32):
        for c in range(4):
            picked_ref[16 * leaf : 16 * leaf + 16, 128 * c : 128 * c + 128] = (
                coeff_ref[0, links_ref[2 * c, leaf] & 127]
                + coeff_ref[1, links_ref[2 * c + 1, leaf] & 127]
            )
    spread_ref[...] = dot(picked_ref[...], split).astype(BF16)
    for copy in copies[1:]:
        copy.wait()
    half = low_half(64)
    row, col = iota((64, 256), 0), iota((64, 256), 1)
    even = (iota((64, 128), 0) & 1) == 0

    def node(n):
        return rows_ref[pl.ds(pl.multiple_of((own[n] - 16) * 64, 64), 64), :]

    carried = [None, (node(0), None)]
    for n in (1, 2):
        high, low = carried[n]
        longer = dot(high[:, :64], node(n))
        if low is not None:
            longer = longer + dot(low[:, :64], node(n))
        carried.append(pieces(longer))
    lo192 = low_half(192)
    for n in range(4):
        pick = jnp.where(((row >> 1) == (col >> 3)) & ((col & 7) == (own[n] & 7)), 1.0, 0.0).astype(BF16)
        blocks = []
        for c in range(3):
            raw = dot(pick, node_coupling_ref[n, c])
            blocks.append(jnp.where(half == even, raw, swap(raw)))
        blocks = jnp.where(lo192, jnp.concatenate(blocks, axis=0), 0.0)
        if n == 0:
            rows = blocks
        else:
            blocks = blocks.astype(BF16)
            high, low = carried[n]
            full = dot_t(blocks, jnp.concatenate([high, high], axis=0))
            if low is not None:
                full = full + dot_t(blocks, jnp.concatenate([low, low], axis=0))
            upper = full.astype(BF16).astype(F32)
            rows = jnp.where(lo192, upper, full - upper)
        coupled_ref[256 * n : 256 * n + 192, :] = rows.astype(BF16)
        coupled_ref[256 * n + 192 : 256 * n + 256, :] = jnp.zeros((64, 128), BF16)

    for j in range(TILES):
        rows = spread_ref[32 * j : 32 * j + 32, :]
        both = dot(
            jnp.concatenate([rows[:, :256], rows[:, 256:]], axis=0),
            jnp.concatenate([coupling_ref[2 * j], coupling_ref[2 * j + 1]], axis=1),
        )
        a = jnp.concatenate([both[:16, :128], both[32:48, :128]], axis=0)
        b = jnp.concatenate([both[16:32, 128:], both[48:, 128:]], axis=0)
        far = jnp.where(lo, a[:16] + swap(a[16:]), swap(b[:16]) + b[16:]).astype(BF16)
        rows = basis_ref[64 * j : 64 * j + 64, :]
        blocks = jnp.concatenate([jnp.where(half, rows, blank), jnp.where(half, blank, rows)], axis=0)
        field_ref[:, 128 * j : 128 * j + 128] = tile(near_ref, j) + dot_t(far, blocks)


def downward_kernel(
    node_links_ref, sides_ref, cross_ref, message_ref,
    field_ref, carry_ref, edge_ref, nodes_ref, coupled_ref,
    out_ref,
    table_ref,
):
    branch, sub = lax.axis_index("leaf"), lax.axis_index("sub")
    lo = low_half(16)
    lo8 = low_half(8)
    lo32 = low_half(32)

    zeros = jnp.zeros((16, 128), BF16)

    def weights(k):
        return nodes_ref[pl.ds(pl.multiple_of(128 * (k - 8), 128), 128), :]

    for q in range(32):
        one, two = message_ref[2 * q].astype(F32), message_ref[2 * q + 1].astype(F32)
        pair = jnp.concatenate(
            [jnp.where(lo8, one, swap(two)), jnp.where(lo8, swap(one), two)], axis=0
        )
        value = dot(pair.astype(BF16), nodes_ref[128 * (q + 24) : 128 * (q + 24) + 128, :])
        table_ref[q] = jnp.concatenate(pieces(value), axis=0)

    def leaf_node(k):
        one = message_ref[k - 64].astype(F32)
        other = swap(one)
        rows = jnp.concatenate([jnp.where(lo8, one, other), jnp.where(lo8, other, one)], axis=0)
        return jnp.concatenate([rows.astype(BF16), zeros], axis=0)

    def parent(k, children):
        value = dot(jnp.where(lo32, *children), weights(k))
        return jnp.concatenate(pieces(value[:16] + value[16:]), axis=0)

    ends = [[node_links_ref[m, (64 >> n) + (branch >> n)] for m in range(3)] for n in range(4)]
    sixteen = ends[2] + [2 * k + m for k in ends[3] for m in range(2)]
    values = [parent(k, [table_ref[2 * k - 32], table_ref[2 * k - 31]]) for k in sixteen]
    found = [
        [leaf_node(k) for k in ends[0]],
        [table_ref[k - 32] for k in ends[1]],
        values[:3],
        [parent(k, values[3 + 2 * n : 5 + 2 * n]) for n, k in enumerate(ends[3])],
    ]
    sources = []
    for a, b, c in found:
        sources += [jnp.where(lo32, a, b), c]
    down = dot(jnp.concatenate(sources, axis=1), coupled_ref[...])
    down = down[:16] + down[16:]
    down = (down + swap(down)).astype(BF16)
    shared = dot(down[:, :64], carry_ref[...])
    left = jnp.where(lo, zeros, jnp.where(sub == 0, cross_ref[...], sides_ref[0]))
    right = jnp.where(lo, jnp.where(sub == 3, cross_ref[...], sides_ref[1]), zeros)
    for j in range(TILES):
        out = shared[:, 128 * j : 128 * j + 128] + tile(field_ref, j)
        if j == 0:
            out = out + dot_t(left, edge_ref[0])
        if j == 15:
            out = out + dot_t(right, edge_ref[1])
        out_ref[:, 128 * j : 128 * j + 128] = out.astype(BF16)


VMEM = pl.BlockSpec(memory_space=pltpu.VMEM)
HBM = pl.BlockSpec(memory_space=pltpu.HBM)
SMEM = pl.BlockSpec(memory_space=pltpu.SMEM)


def shape(dims, dtype=BF16):
    return jax.ShapeDtypeStruct(dims, dtype)


def pinned(dims, dtype=BF16):
    return pltpu.VMEM(dims, dtype)


def stays(x):
    return pltpu.with_memory_space_constraint(x, pltpu.HBM)


def near_by(x):
    return pltpu.with_memory_space_constraint(x, pltpu.VMEM)


def call(kernel, name, outs, in_specs, out_specs, scratch, size, mib, aliases={}):
    return pl.pallas_call(
        kernel,
        out_shape=outs,
        in_specs=in_specs,
        out_specs=out_specs,
        scratch_shapes=scratch,
        compiler_params=pltpu.CompilerParams(vmem_limit_bytes=mib << 20),
        cost_estimate=pl.CostEstimate(flops=10**9, bytes_accessed=size, transcendentals=0),
        input_output_aliases=aliases,
        name=name,
    )


def dma(count):
    return pltpu.SemaphoreType.DMA((count,))


def upward(*args):
    return call(
        upward_kernel, "upward",
        [
            shape((16, PAYLOAD)), pinned((16, 2048)), pinned((32, 128), I32), pinned((4, 256, 128)),
            pinned((4, 256, 128)), pinned((3, 4, 256, 128)), pinned((14, 256, 128)), pinned((8, 32), I32),
        ],
        [HBM] * 7, [VMEM] * 8,
        [
            pltpu.SMEM((32,), I32),
            pltpu.VMEM((16, 2048), BF16),
            pltpu.VMEM((512, 512), BF16),
            dma(7),
        ],
        10**6, 8,
    )(*args)


def near_field(*args):
    return call(
        near_kernel, "near",
        [
            pinned((16, 2048), F32), pinned((1024, 128)), pinned((1024, 128)), pinned((2, 128, 128)),
            pinned((16, 128)),
            pinned((56 * 128, 128)),
        ],
        [VMEM] * 7, [VMEM] * 6,
        [
            pltpu.VMEM((16, 18 * 128), BF16),
            pltpu.VMEM((8, 512, 128), F32),
            pltpu.VMEM((4, 512, 128), F32),
        ],
        3 * 10**6, 12,
    )(*args)


def message(*args):
    return call(
        message_kernel, "message", [shape((64, 8, 128)), shape((16, 128)), shape((2, 16, 128))], [VMEM] * 4, [VMEM] * 3, [],
        10**5, 4,
    )(*args)


def middle(*args):
    return call(
        middle_kernel, "middle",
        [pinned((1024, 128)), pinned((16, 2048), F32), pinned((64, 2048)), pltpu.SMEM((3, 128), I32)],
        [HBM, VMEM, HBM, HBM] + [VMEM] * 8, [VMEM] * 3 + [SMEM],
        [
            pltpu.SMEM((8, 32), I32),
            pltpu.VMEM((4, 3, 256, 128), BF16),
            pltpu.VMEM((32, 256, 128), BF16),
            pltpu.VMEM((2, 128, 16, 128), BF16),
            pltpu.VMEM((512, 512), BF16),
            pltpu.VMEM((512, 512), BF16),
            dma(10),
        ],
        6 * 10**6, 16, {9: 1},
    )(*args)


def downward(*args):
    return call(
        downward_kernel, "downward", shape((16, 2048)), [SMEM] + [VMEM] * 8, VMEM,
        [pltpu.VMEM((32, 32, 128), BF16)],
        4 * 10**6, 8,
    )(*args)


def grouped(table):
    lead, rows = table.shape[:-2], table.shape[-2]
    table = jnp.swapaxes(table.reshape(*lead, rows // 8, 8, 32, 128), -3, -2)
    return table.reshape(*lead, rows // 8, 256, 128)


def body(
    vectors, leaf_size, leaf_basis, near_blocks, leaf_links, leaf_coupling, leaf_transfer,
    node_transfer, node_links, node_coupling,
):
    basis, transfer, nodes = grouped(leaf_basis), grouped(leaf_transfer), grouped(node_transfer)
    coupling = grouped(leaf_coupling)[:, 0]
    near = grouped(near_blocks.transpose(1, 0, 2))
    node_coupled = grouped(node_coupling.transpose(1, 0, 2))

    basis, transfer, nodes, coupling, near, node_coupled, vectors, leaf_size, links, node_links = map(
        stays,
        (
            basis, transfer, nodes, coupling, near, node_coupled, vectors, leaf_size, leaf_links.T,
            node_links.T,
        ),
    )
    payload, *tables = upward(leaf_size, vectors, basis, transfer, near, nodes, links)
    kept_points, limits, basis, transfer, near, nodes, links = map(near_by, tables)
    others = [
        lax.ppermute(payload, "sub", [(s, s ^ d) for s in range(4)]) for d in (1, 2, 3)
    ]
    near_part, basis_p, carry, edge, share, nodes_p = near_field(
        kept_points, limits, near, basis, transfer, nodes, payload
    )
    messages, cross, sides = message(share, *others)
    summed = lax.all_to_all(messages, "leaf", 0, 0)

    branches = lax.axis_size("leaf")
    routes = [(4 * b, 4 * b + 4) for b in range(branches - 1)]
    routes += [(4 * b + 3, 4 * b - 1) for b in range(1, branches)]
    cross = lax.ppermute(cross, ("leaf", "sub"), routes)

    coupled, field, turned, partners = middle(
        node_coupled, links, node_links, coupling, near_by(nodes_p), payload, others[1], others[2], others[0],
        near_by(near_part), near_by(basis_p), near_by(carry),
    )
    return downward(
        pltpu.with_memory_space_constraint(partners, pltpu.SMEM), sides, cross, summed,
        *map(near_by, (field, turned, edge, nodes_p, coupled)),
    )


def solution(mesh):
    split = ("leaf", "sub")
    placed = (
        P(None, split), P(split), P(split, None), P(split, None, None), P(split, None),
        P(split, None, None), P(split, None), P(), P(), P(),
    )
    return jax.shard_map(
        body, mesh=mesh, in_specs=placed, out_specs=P(None, split), check_vma=False
    )
```

```python
import jax
import jax.numpy as jnp
from jax import lax
from jax.experimental import pallas as pl
from jax.experimental.pallas import tpu as pltpu
from jax.sharding import PartitionSpec as P

F32, BF16, I32 = jnp.float32, jnp.bfloat16, jnp.int32
TILES = 16
COEFF = 16 * 128
PAYLOAD = 19 * 128


def iota(shape, dim):
    return lax.broadcasted_iota(I32, shape, dim)


def dot(a, b):
    return jnp.dot(a, b, preferred_element_type=F32)


def dot_t(a, b):
    return lax.dot_general(a, b, (((1,), (1,)), ((), ())), preferred_element_type=F32)


def swap(x):
    return pltpu.roll(x, 64, 1)


def low_half(rows):
    return iota((rows, 128), 1) < 64


def tile(ref, j):
    return ref[:, 128 * j : 128 * j + 128]


def pieces(x):
    high = x.astype(BF16)
    return high, (x - high.astype(F32)).astype(BF16)


def split_map():
    row = iota((512, 128), 0)
    rank = row & 63
    target = (rank & 1) * 256 + (rank >> 1) * 8 + (row >> 6) - iota((512, 128), 1)
    return jnp.concatenate(
        [jnp.where(target == 128 * q, 1.0, 0.0).astype(BF16) for q in range(4)], axis=1
    )


def group_map():
    row, col = iota((256, 256), 0), iota((256, 256), 1)
    return jnp.where(col == (row & 31) * 8 + (row >> 5), 1.0, 0.0).astype(BF16)


def plain_rows(raw, rows_ref):
    count = raw.shape[0]
    lo = low_half(count)
    other = swap(raw)
    rows_ref[pl.ds(0, count, stride=2), :] = jnp.where(lo, raw, other)
    rows_ref[pl.ds(1, count, stride=2), :] = jnp.where(lo, other, raw)


def present(size_ref, j):
    lane = iota((16, 128), 1)
    limit = jnp.where(lane < 64, size_ref[2 * j], size_ref[2 * j + 1])
    return (lane & 63) < limit


def kept(size_ref, x_ref, j):
    return jnp.where(present(size_ref, j), tile(x_ref, j).astype(F32), 0.0)


def start_all(sems, pairs):
    copies = [pltpu.make_async_copy(a, b, sems.at[n]) for n, (a, b) in enumerate(pairs)]
    for copy in copies:
        copy.start()
    return copies


def upward_kernel(
    size_hbm, x_hbm, basis_hbm, transfer_hbm, near_hbm, nodes_hbm, links_hbm,
    pay_ref, small_ref, masked_ref, limits_ref, basis_ref, transfer_ref, near_ref, nodes_ref, links_ref,
    size_ref, x_ref, map_ref, sems,
):
    copies = start_all(
        sems,
        [
            (x_hbm, x_ref), (size_hbm, size_ref), (basis_hbm, basis_ref), (transfer_hbm, transfer_ref),
            (near_hbm, near_ref), (nodes_hbm.at[pl.ds(2, 14)], nodes_ref), (links_hbm, links_ref),
        ],
    )
    lo = low_half(16)
    map_ref[...] = split_map()
    copies[0].wait()
    copies[1].wait()
    for j in range(TILES):
        masked_ref[:, 128 * j : 128 * j + 128] = kept(size_ref, x_ref, j).astype(BF16)
    points = jnp.concatenate([masked_ref[:, 512 * g : 512 * g + 512] for g in range(4)], axis=0)
    spread = dot(points, map_ref[...]).astype(BF16)
    member = iota((16, 256), 1) & 7
    picks = [jnp.where(member == m, 1.0, 0.0).astype(BF16) for m in range(8)]
    copies[2].wait()
    for g in range(4):
        halves = [spread[16 * g : 16 * g + 16, 256 * h : 256 * h + 256] for h in range(2)]
        rows = jnp.concatenate([halves[h] * picks[m] for m in range(8) for h in range(2)], axis=0)
        out = dot(rows, basis_ref[g])
        for q in range(4):
            a0, a1, b0, b1 = [out[64 * q + 16 * n : 64 * q + 16 * n + 16] for n in range(4)]
            coeff = jnp.where(lo, a0 + swap(a1), swap(b0) + b1)
            j = 4 * g + q
            pay_ref[:, 128 * j : 128 * j + 128] = coeff.astype(BF16)
    coeffs = jnp.concatenate([pay_ref[:, 512 * g : 512 * g + 512] for g in range(4)], axis=0)
    spread = dot(coeffs, map_ref[...]).astype(BF16)
    copies[3].wait()
    total = jnp.zeros((32, 128), F32)
    for g in range(4):
        rows = jnp.concatenate(
            [spread[16 * g : 16 * g + 16, 256 * h : 256 * h + 256] for h in range(2)], axis=0
        )
        total = total + dot(rows, transfer_ref[g])
    share = jnp.where(lo, total[:16] + swap(total[16:]), swap(total[:16]) + total[16:])
    packed = jnp.where(low_half(8), share[:8], share[8:])
    high = packed.astype(BF16).astype(F32)
    pay_ref[:, COEFF : COEFF + 128] = jnp.concatenate([high, packed - high], axis=0).astype(BF16)
    pay_ref[:, COEFF + 128 : COEFF + 256] = tile(masked_ref, 0)
    pay_ref[:, COEFF + 256 : COEFF + 384] = tile(masked_ref, 15)
    small_ref[...] = tile(pay_ref, 16)
    for n in range(32):
        limits_ref[n : n + 1, :] = jnp.full((1, 128), size_ref[n], I32)
    for copy in copies[4:]:
        copy.wait()


def near_kernel(
    kept_ref, limits_ref, near_ref, basis_ref, transfer_ref, nodes_ref, pay_ref,
    field_ref, basis_rows, carry_rows, edge_ref, share_ref, node_rows,
    masked_ref, raw_ref, node_raw,
):
    share_ref[...] = tile(pay_ref, 16)
    lane = iota((16, 128), 1)
    collect = group_map()
    half = low_half(64)
    row = iota((64, 128), 0)
    for g in range(4):
        raw = dot(collect, jnp.concatenate([basis_ref[g], transfer_ref[g]], axis=1))
        for n in range(2):
            plain_rows(raw[:, 128 * n : 128 * n + 128], raw_ref.at[2 * g + n])
        for q in range(4):
            j = 4 * g + q
            pair = [raw_ref[2 * g, 128 * q + 64 * m : 128 * q + 64 * m + 64, :] for m in range(2)]
            pair = [jnp.where(row < limits_ref[2 * j + m : 2 * j + m + 1, :], pair[m], 0.0) for m in range(2)]
            start = 64 * j
            basis_rows[start : start + 64, :] = jnp.where(half, *pair).astype(BF16)
            blocks = jnp.concatenate([jnp.where(half, pair[0], 0.0), jnp.where(half, 0.0, pair[1])], axis=0)
            carry = dot(blocks.astype(BF16), raw_ref[2 * g + 1, 128 * q : 128 * q + 128, :].astype(BF16))
            carry_rows[start : start + 64, :] = jnp.where(half, carry[:64], carry[64:]).astype(BF16)
    masked_ref[:, 0:128] = jnp.zeros((16, 128), BF16)
    masked_ref[:, 17 * 128 : 18 * 128] = jnp.zeros((16, 128), BF16)
    masked_ref[:, 128 : 17 * 128] = kept_ref[...]
    lo = low_half(16)
    for pair in range(2):
        for s in range(3):
            raw = dot(
                collect, jnp.concatenate([near_ref[s, 2 * pair], near_ref[s, 2 * pair + 1]], axis=1)
            )
            for n in range(2):
                plain_rows(raw[:, 128 * n : 128 * n + 128], raw_ref.at[3 * n + s])
        for q in range(8):
            j = 8 * pair + q
            at = 128 * (q % 4)
            a = [raw_ref[3 * (q // 4) + s, at : at + 64, :] for s in range(3)]
            b = [raw_ref[3 * (q // 4) + s, at + 64 : at + 128, :] for s in range(3)]
            inner = jnp.concatenate([jnp.where(half, a[1], a[2]), jnp.where(half, b[0], b[1])], axis=0)
            outer = jnp.concatenate([jnp.where(half, 0.0, a[0]), jnp.where(half, b[2], 0.0)], axis=0)
            if j in (0, 15):
                edge = jnp.concatenate(
                    [
                        jnp.where(row < limits_ref[2 * j + m : 2 * j + m + 1, :], outer[64 * m : 64 * m + 64], 0.0)
                        for m in range(2)
                    ],
                    axis=0,
                )
                edge_ref[j // 15] = edge.astype(BF16)
            outer = outer.astype(BF16)
            around = jnp.where(lo, tile(masked_ref, j + 2), tile(masked_ref, j))
            near = dot_t(
                jnp.concatenate([tile(masked_ref, j + 1), around], axis=1),
                jnp.concatenate([inner.astype(BF16), outer], axis=1),
            )
            field_ref[:, 128 * j : 128 * j + 128] = jnp.where(
                (lane & 63) < jnp.where(lane < 64, limits_ref[2 * j : 2 * j + 1, :], limits_ref[2 * j + 1 : 2 * j + 2, :]),
                near,
                0.0,
            )
    for g in range(0, 14, 2):
        raw = dot(collect, jnp.concatenate([nodes_ref[g], nodes_ref[g + 1]], axis=1))
        for n in range(2):
            plain_rows(raw[:, 128 * n : 128 * n + 128], node_raw.at[(g + n) % 4])
            node_rows[512 * (g + n) : 512 * (g + n) + 512, :] = node_raw[(g + n) % 4].astype(BF16)


def message_kernel(
    share_ref, one_ref, two_ref, three_ref, own_ref, out_ref, cross_ref, sides_ref, again_ref
):
    total = share_ref[...].astype(F32)
    for ref, at in ((one_ref, 16), (two_ref, 0), (three_ref, 16)):
        total = total + tile(ref, at).astype(F32)
    again_ref[...] = own_ref[:, :COEFF]
    packed = (total[:8] + total[8:]).astype(BF16)
    for n in range(64):
        out_ref[n] = packed
    sub = lax.axis_index("sub")
    cross_ref[...] = jnp.where(sub == 0, tile(three_ref, 18), tile(three_ref, 17))
    sides_ref[0] = jnp.where(sub == 2, tile(three_ref, 18), tile(one_ref, 18))
    sides_ref[1] = jnp.where(sub == 1, tile(three_ref, 17), tile(one_ref, 17))


def middle_kernel(
    node_coupling_hbm, links_vmem, node_links_hbm, coupling_hbm, rows_ref,
    own_ref, two_ref, three_ref, one_ref, near_ref, basis_ref, carry_rows,
    coupled_ref, field_ref, carry_ref, node_links_ref,
    links_ref, node_coupling_ref, coupling_ref, coeff_ref, picked_ref, spread_ref, sems,
):
    branch = lax.axis_index("leaf")
    own = [64 + branch, 32 + (branch >> 1), 16 + (branch >> 2), 8 + (branch >> 3)]
    sources = (own_ref, one_ref, two_ref, three_ref)
    copies = start_all(
        sems,
        [(links_vmem, links_ref)]
        + [(coupling_hbm.at[pl.ds(8 * n, 8)], coupling_ref.at[pl.ds(8 * n, 8)]) for n in range(4)]
        + [(node_coupling_hbm.at[:, own[n] >> 3], node_coupling_ref.at[n]) for n in range(4)]
        + [(node_links_hbm, node_links_ref)],
    )
    split = split_map()
    unit = jnp.where(iota((128, 128), 0) == iota((128, 128), 1), 1.0, 0.0).astype(BF16)
    for j in range(TILES):
        rows = carry_rows[64 * j : 64 * j + 64, :]
        turned = dot_t(unit, jnp.concatenate([rows, rows], axis=0))
        carry_ref[:, 128 * j : 128 * j + 128] = jnp.where(low_half(64), turned[:64], turned[64:]).astype(BF16)
    lo = low_half(16)
    nothing = jnp.zeros((16, 128), BF16)
    half = low_half(64)
    blank = jnp.zeros((64, 128), BF16)
    sub = lax.axis_index("sub")
    for d, ref in enumerate(sources):
        first = (sub ^ d) * 32
        for j in range(TILES):
            x = tile(ref, j)
            y = swap(x)
            for m, (a, b) in enumerate(((x, y), (y, x))):
                coeff_ref[0, first + 2 * j + m] = jnp.where(lo, a, nothing)
                coeff_ref[1, first + 2 * j + m] = jnp.where(lo, nothing, b)
    copies[0].wait()
    for leaf in range(32):
        for c in range(4):
            picked_ref[16 * leaf : 16 * leaf + 16, 128 * c : 128 * c + 128] = (
                coeff_ref[0, links_ref[2 * c, leaf] & 127]
                + coeff_ref[1, links_ref[2 * c + 1, leaf] & 127]
            )
    spread_ref[...] = dot(picked_ref[...], split).astype(BF16)
    for copy in copies[1:]:
        copy.wait()
    half = low_half(64)
    row, col = iota((64, 256), 0), iota((64, 256), 1)
    even = (iota((64, 128), 0) & 1) == 0

    def node(n):
        return rows_ref[pl.ds(pl.multiple_of((own[n] - 16) * 64, 64), 64), :]

    carried = [None, (node(0), None)]
    for n in (1, 2):
        high, low = carried[n]
        longer = dot(high[:, :64], node(n))
        if low is not None:
            longer = longer + dot(low[:, :64], node(n))
        carried.append(pieces(longer))
    lo192 = low_half(192)
    for n in range(4):
        pick = jnp.where(((row >> 1) == (col >> 3)) & ((col & 7) == (own[n] & 7)), 1.0, 0.0).astype(BF16)
        blocks = []
        for c in range(3):
            raw = dot(pick, node_coupling_ref[n, c])
            blocks.append(jnp.where(half == even, raw, swap(raw)))
        blocks = jnp.where(lo192, jnp.concatenate(blocks, axis=0), 0.0)
        if n == 0:
            rows = blocks
        else:
            blocks = blocks.astype(BF16)
            high, low = carried[n]
            full = dot_t(blocks, jnp.concatenate([high, high], axis=0))
            if low is not None:
                full = full + dot_t(blocks, jnp.concatenate([low, low], axis=0))
            upper = full.astype(BF16).astype(F32)
            rows = jnp.where(lo192, upper, full - upper)
        coupled_ref[256 * n : 256 * n + 192, :] = rows.astype(BF16)
        coupled_ref[256 * n + 192 : 256 * n + 256, :] = jnp.zeros((64, 128), BF16)

    for j in range(TILES):
        rows = spread_ref[32 * j : 32 * j + 32, :]
        both = dot(
            jnp.concatenate([rows[:, :256], rows[:, 256:]], axis=0),
            jnp.concatenate([coupling_ref[2 * j], coupling_ref[2 * j + 1]], axis=1),
        )
        a = jnp.concatenate([both[:16, :128], both[32:48, :128]], axis=0)
        b = jnp.concatenate([both[16:32, 128:], both[48:, 128:]], axis=0)
        far = jnp.where(lo, a[:16] + swap(a[16:]), swap(b[:16]) + b[16:]).astype(BF16)
        rows = basis_ref[64 * j : 64 * j + 64, :]
        blocks = jnp.concatenate([jnp.where(half, rows, blank), jnp.where(half, blank, rows)], axis=0)
        field_ref[:, 128 * j : 128 * j + 128] = tile(near_ref, j) + dot_t(far, blocks)


def downward_kernel(
    node_links_ref, sides_ref, cross_ref, message_ref,
    field_ref, carry_ref, edge_ref, nodes_ref, coupled_ref,
    out_ref,
    table_ref,
):
    branch, sub = lax.axis_index("leaf"), lax.axis_index("sub")
    lo = low_half(16)
    lo8 = low_half(8)
    lo32 = low_half(32)

    zeros = jnp.zeros((16, 128), BF16)

    def weights(k):
        return nodes_ref[pl.ds(pl.multiple_of(128 * (k - 8), 128), 128), :]

    for q in range(32):
        one, two = message_ref[2 * q].astype(F32), message_ref[2 * q + 1].astype(F32)
        pair = jnp.concatenate(
            [jnp.where(lo8, one, swap(two)), jnp.where(lo8, swap(one), two)], axis=0
        )
        value = dot(pair.astype(BF16), nodes_ref[128 * (q + 24) : 128 * (q + 24) + 128, :])
        table_ref[q] = jnp.concatenate(pieces(value), axis=0)

    def leaf_node(k):
        one = message_ref[k - 64].astype(F32)
        other = swap(one)
        rows = jnp.concatenate([jnp.where(lo8, one, other), jnp.where(lo8, other, one)], axis=0)
        return jnp.concatenate([rows.astype(BF16), zeros], axis=0)

    def parent(k, children):
        value = dot(jnp.where(lo32, *children), weights(k))
        return jnp.concatenate(pieces(value[:16] + value[16:]), axis=0)

    ends = [[node_links_ref[m, (64 >> n) + (branch >> n)] for m in range(3)] for n in range(4)]
    sixteen = ends[2] + [2 * k + m for k in ends[3] for m in range(2)]
    values = [parent(k, [table_ref[2 * k - 32], table_ref[2 * k - 31]]) for k in sixteen]
    found = [
        [leaf_node(k) for k in ends[0]],
        [table_ref[k - 32] for k in ends[1]],
        values[:3],
        [parent(k, values[3 + 2 * n : 5 + 2 * n]) for n, k in enumerate(ends[3])],
    ]
    sources = []
    for a, b, c in found:
        sources += [jnp.where(lo32, a, b), c]
    down = dot(jnp.concatenate(sources, axis=1), coupled_ref[...])
    down = down[:16] + down[16:]
    down = (down + swap(down)).astype(BF16)
    shared = dot(down[:, :64], carry_ref[...])
    left = jnp.where(lo, zeros, jnp.where(sub == 0, cross_ref[...], sides_ref[0]))
    right = jnp.where(lo, jnp.where(sub == 3, cross_ref[...], sides_ref[1]), zeros)
    for j in range(TILES):
        out = shared[:, 128 * j : 128 * j + 128] + tile(field_ref, j)
        if j == 0:
            out = out + dot_t(left, edge_ref[0])
        if j == 15:
            out = out + dot_t(right, edge_ref[1])
        out_ref[:, 128 * j : 128 * j + 128] = out.astype(BF16)


VMEM = pl.BlockSpec(memory_space=pltpu.VMEM)
HBM = pl.BlockSpec(memory_space=pltpu.HBM)
SMEM = pl.BlockSpec(memory_space=pltpu.SMEM)


def shape(dims, dtype=BF16):
    return jax.ShapeDtypeStruct(dims, dtype)


def pinned(dims, dtype=BF16):
    return pltpu.VMEM(dims, dtype)


def stays(x):
    return pltpu.with_memory_space_constraint(x, pltpu.HBM)


def near_by(x):
    return pltpu.with_memory_space_constraint(x, pltpu.VMEM)


def call(kernel, name, outs, in_specs, out_specs, scratch, size, mib, aliases={}):
    return pl.pallas_call(
        kernel,
        out_shape=outs,
        in_specs=in_specs,
        out_specs=out_specs,
        scratch_shapes=scratch,
        compiler_params=pltpu.CompilerParams(vmem_limit_bytes=mib << 20),
        cost_estimate=pl.CostEstimate(flops=10**9, bytes_accessed=size, transcendentals=0),
        input_output_aliases=aliases,
        name=name,
    )


def dma(count):
    return pltpu.SemaphoreType.DMA((count,))


def upward(*args):
    return call(
        upward_kernel, "upward",
        [
            shape((16, PAYLOAD)), shape((16, 128)), pinned((16, 2048)), pinned((32, 128), I32), pinned((4, 256, 128)),
            pinned((4, 256, 128)), pinned((3, 4, 256, 128)), pinned((14, 256, 128)), pinned((8, 32), I32),
        ],
        [HBM] * 7, [VMEM] * 9,
        [
            pltpu.SMEM((32,), I32),
            pltpu.VMEM((16, 2048), BF16),
            pltpu.VMEM((512, 512), BF16),
            dma(7),
        ],
        10**6, 8,
    )(*args)


def near_field(*args):
    return call(
        near_kernel, "near",
        [
            pinned((16, 2048), F32), pinned((1024, 128)), pinned((1024, 128)), pinned((2, 128, 128)),
            pinned((16, 128)),
            pinned((56 * 128, 128)),
        ],
        [VMEM] * 7, [VMEM] * 6,
        [
            pltpu.VMEM((16, 18 * 128), BF16),
            pltpu.VMEM((8, 512, 128), F32),
            pltpu.VMEM((4, 512, 128), F32),
        ],
        3 * 10**6, 12,
    )(*args)


def message(*args):
    return call(
        message_kernel, "message", [shape((64, 8, 128)), shape((16, 128)), shape((2, 16, 128)), shape((16, COEFF))],
        [VMEM] * 5, [VMEM] * 4, [],
        10**5, 4,
    )(*args)


def middle(*args):
    return call(
        middle_kernel, "middle",
        [pinned((1024, 128)), pinned((16, 2048), F32), pinned((64, 2048)), pltpu.SMEM((3, 128), I32)],
        [HBM, VMEM, HBM, HBM] + [VMEM] * 8, [VMEM] * 3 + [SMEM],
        [
            pltpu.SMEM((8, 32), I32),
            pltpu.VMEM((4, 3, 256, 128), BF16),
            pltpu.VMEM((32, 256, 128), BF16),
            pltpu.VMEM((2, 128, 16, 128), BF16),
            pltpu.VMEM((512, 512), BF16),
            pltpu.VMEM((512, 512), BF16),
            dma(10),
        ],
        6 * 10**6, 16, {9: 1},
    )(*args)


def downward(*args):
    return call(
        downward_kernel, "downward", shape((16, 2048)), [SMEM] + [VMEM] * 8, VMEM,
        [pltpu.VMEM((32, 32, 128), BF16)],
        4 * 10**6, 8,
    )(*args)


def grouped(table):
    lead, rows = table.shape[:-2], table.shape[-2]
    table = jnp.swapaxes(table.reshape(*lead, rows // 8, 8, 32, 128), -3, -2)
    return table.reshape(*lead, rows // 8, 256, 128)


def body(
    vectors, leaf_size, leaf_basis, near_blocks, leaf_links, leaf_coupling, leaf_transfer,
    node_transfer, node_links, node_coupling,
):
    basis, transfer, nodes = grouped(leaf_basis), grouped(leaf_transfer), grouped(node_transfer)
    coupling = grouped(leaf_coupling)[:, 0]
    near = grouped(near_blocks.transpose(1, 0, 2))
    node_coupled = grouped(node_coupling.transpose(1, 0, 2))

    basis, transfer, nodes, coupling, near, node_coupled, vectors, leaf_size, links, node_links = map(
        stays,
        (
            basis, transfer, nodes, coupling, near, node_coupled, vectors, leaf_size, leaf_links.T,
            node_links.T,
        ),
    )
    payload, small, *tables = upward(leaf_size, vectors, basis, transfer, near, nodes, links)
    kept_points, limits, basis, transfer, near, nodes, links = map(near_by, tables)
    others = [
        lax.ppermute(small if d == 2 else payload, "sub", [(s, s ^ d) for s in range(4)])
        for d in (1, 2, 3)
    ]
    near_part, basis_p, carry, edge, share, nodes_p = near_field(
        kept_points, limits, near, basis, transfer, nodes, payload
    )
    messages, cross, sides, again = message(share, *others, payload)
    opposite = lax.ppermute(again, "sub", [(s, s ^ 2) for s in range(4)])
    summed = lax.all_to_all(messages, "leaf", 0, 0)

    branches = lax.axis_size("leaf")
    routes = [(4 * b, 4 * b + 4) for b in range(branches - 1)]
    routes += [(4 * b + 3, 4 * b - 1) for b in range(1, branches)]
    cross = lax.ppermute(cross, ("leaf", "sub"), routes)

    coupled, field, turned, partners = middle(
        node_coupled, links, node_links, coupling, near_by(nodes_p), payload, opposite, others[2], others[0],
        near_by(near_part), near_by(basis_p), near_by(carry),
    )
    return downward(
        pltpu.with_memory_space_constraint(partners, pltpu.SMEM), sides, cross, summed,
        *map(near_by, (field, turned, edge, nodes_p, coupled)),
    )


def solution(mesh):
    split = ("leaf", "sub")
    placed = (
        P(None, split), P(split), P(split, None), P(split, None, None), P(split, None),
        P(split, None, None), P(split, None), P(), P(), P(),
    )
    return jax.shard_map(
        body, mesh=mesh, in_specs=placed, out_specs=P(None, split), check_vma=False
    )
```

```python
import jax
import jax.numpy as jnp
from jax import lax
from jax.experimental import pallas as pl
from jax.experimental.pallas import tpu as pltpu
from jax.sharding import PartitionSpec as P

F32, BF16, I32 = jnp.float32, jnp.bfloat16, jnp.int32
TILES = 16
COEFF = 16 * 128
PAYLOAD = 19 * 128


def iota(shape, dim):
    return lax.broadcasted_iota(I32, shape, dim)


def dot(a, b):
    return jnp.dot(a, b, preferred_element_type=F32)


def dot_t(a, b):
    return lax.dot_general(a, b, (((1,), (1,)), ((), ())), preferred_element_type=F32)


def swap(x):
    return pltpu.roll(x, 64, 1)


def low_half(rows):
    return iota((rows, 128), 1) < 64


def tile(ref, j):
    return ref[:, 128 * j : 128 * j + 128]


def pieces(x):
    high = x.astype(BF16)
    return high, (x - high.astype(F32)).astype(BF16)


def split_map():
    row = iota((512, 128), 0)
    rank = row & 63
    target = (rank & 1) * 256 + (rank >> 1) * 8 + (row >> 6) - iota((512, 128), 1)
    return jnp.concatenate(
        [jnp.where(target == 128 * q, 1.0, 0.0).astype(BF16) for q in range(4)], axis=1
    )


def group_map():
    row, col = iota((256, 256), 0), iota((256, 256), 1)
    return jnp.where(col == (row & 31) * 8 + (row >> 5), 1.0, 0.0).astype(BF16)


def plain_rows(raw, rows_ref):
    count = raw.shape[0]
    lo = low_half(count)
    other = swap(raw)
    rows_ref[pl.ds(0, count, stride=2), :] = jnp.where(lo, raw, other)
    rows_ref[pl.ds(1, count, stride=2), :] = jnp.where(lo, other, raw)


def present(size_ref, j):
    lane = iota((16, 128), 1)
    limit = jnp.where(lane < 64, size_ref[2 * j], size_ref[2 * j + 1])
    return (lane & 63) < limit


def kept(size_ref, x_ref, j):
    return jnp.where(present(size_ref, j), tile(x_ref, j).astype(F32), 0.0)


def start_all(sems, pairs):
    copies = [pltpu.make_async_copy(a, b, sems.at[n]) for n, (a, b) in enumerate(pairs)]
    for copy in copies:
        copy.start()
    return copies


def upward_kernel(
    size_hbm, x_hbm, basis_hbm, transfer_hbm, near_hbm, nodes_hbm, links_hbm,
    pay_ref, masked_ref, limits_ref, basis_ref, transfer_ref, near_ref, nodes_ref, links_ref,
    size_ref, x_ref, map_ref, sems,
):
    copies = start_all(
        sems,
        [
            (x_hbm, x_ref), (size_hbm, size_ref), (basis_hbm, basis_ref), (transfer_hbm, transfer_ref),
            (near_hbm, near_ref), (nodes_hbm.at[pl.ds(2, 14)], nodes_ref), (links_hbm, links_ref),
        ],
    )
    lo = low_half(16)
    map_ref[...] = split_map()
    copies[0].wait()
    copies[1].wait()
    for j in range(TILES):
        masked_ref[:, 128 * j : 128 * j + 128] = kept(size_ref, x_ref, j).astype(BF16)
    points = jnp.concatenate([masked_ref[:, 512 * g : 512 * g + 512] for g in range(4)], axis=0)
    spread = dot(points, map_ref[...]).astype(BF16)
    member = iota((16, 256), 1) & 7
    picks = [jnp.where(member == m, 1.0, 0.0).astype(BF16) for m in range(8)]
    copies[2].wait()
    for g in range(4):
        halves = [spread[16 * g : 16 * g + 16, 256 * h : 256 * h + 256] for h in range(2)]
        rows = jnp.concatenate([halves[h] * picks[m] for m in range(8) for h in range(2)], axis=0)
        out = dot(rows, basis_ref[g])
        for q in range(4):
            a0, a1, b0, b1 = [out[64 * q + 16 * n : 64 * q + 16 * n + 16] for n in range(4)]
            coeff = jnp.where(lo, a0 + swap(a1), swap(b0) + b1)
            j = 4 * g + q
            pay_ref[:, 128 * j : 128 * j + 128] = coeff.astype(BF16)
    coeffs = jnp.concatenate([pay_ref[:, 512 * g : 512 * g + 512] for g in range(4)], axis=0)
    spread = dot(coeffs, map_ref[...]).astype(BF16)
    copies[3].wait()
    total = jnp.zeros((32, 128), F32)
    for g in range(4):
        rows = jnp.concatenate(
            [spread[16 * g : 16 * g + 16, 256 * h : 256 * h + 256] for h in range(2)], axis=0
        )
        total = total + dot(rows, transfer_ref[g])
    share = jnp.where(lo, total[:16] + swap(total[16:]), swap(total[:16]) + total[16:])
    packed = jnp.where(low_half(8), share[:8], share[8:])
    high = packed.astype(BF16).astype(F32)
    pay_ref[:, COEFF : COEFF + 128] = jnp.concatenate([high, packed - high], axis=0).astype(BF16)
    pay_ref[:, COEFF + 128 : COEFF + 256] = tile(masked_ref, 0)
    pay_ref[:, COEFF + 256 : COEFF + 384] = tile(masked_ref, 15)
    for n in range(32):
        limits_ref[n : n + 1, :] = jnp.full((1, 128), size_ref[n], I32)
    for copy in copies[4:]:
        copy.wait()


def near_kernel(
    kept_ref, limits_ref, near_ref, basis_ref, transfer_ref, nodes_ref, pay_ref,
    field_ref, basis_rows, carry_rows, edge_ref, share_ref, node_rows,
    masked_ref, raw_ref, node_raw,
):
    share_ref[...] = tile(pay_ref, 16)
    lane = iota((16, 128), 1)
    collect = group_map()
    half = low_half(64)
    row = iota((64, 128), 0)
    for g in range(4):
        raw = dot(collect, jnp.concatenate([basis_ref[g], transfer_ref[g]], axis=1))
        for n in range(2):
            plain_rows(raw[:, 128 * n : 128 * n + 128], raw_ref.at[2 * g + n])
        for q in range(4):
            j = 4 * g + q
            pair = [raw_ref[2 * g, 128 * q + 64 * m : 128 * q + 64 * m + 64, :] for m in range(2)]
            pair = [jnp.where(row < limits_ref[2 * j + m : 2 * j + m + 1, :], pair[m], 0.0) for m in range(2)]
            start = 64 * j
            basis_rows[start : start + 64, :] = jnp.where(half, *pair).astype(BF16)
            blocks = jnp.concatenate([jnp.where(half, pair[0], 0.0), jnp.where(half, 0.0, pair[1])], axis=0)
            carry = dot(blocks.astype(BF16), raw_ref[2 * g + 1, 128 * q : 128 * q + 128, :].astype(BF16))
            carry_rows[start : start + 64, :] = jnp.where(half, carry[:64], carry[64:]).astype(BF16)
    masked_ref[:, 0:128] = jnp.zeros((16, 128), BF16)
    masked_ref[:, 17 * 128 : 18 * 128] = jnp.zeros((16, 128), BF16)
    masked_ref[:, 128 : 17 * 128] = kept_ref[...]
    lo = low_half(16)
    for pair in range(2):
        for s in range(3):
            raw = dot(
                collect, jnp.concatenate([near_ref[s, 2 * pair], near_ref[s, 2 * pair + 1]], axis=1)
            )
            for n in range(2):
                plain_rows(raw[:, 128 * n : 128 * n + 128], raw_ref.at[3 * n + s])
        for q in range(8):
            j = 8 * pair + q
            at = 128 * (q % 4)
            a = [raw_ref[3 * (q // 4) + s, at : at + 64, :] for s in range(3)]
            b = [raw_ref[3 * (q // 4) + s, at + 64 : at + 128, :] for s in range(3)]
            inner = jnp.concatenate([jnp.where(half, a[1], a[2]), jnp.where(half, b[0], b[1])], axis=0)
            outer = jnp.concatenate([jnp.where(half, 0.0, a[0]), jnp.where(half, b[2], 0.0)], axis=0)
            if j in (0, 15):
                edge = jnp.concatenate(
                    [
                        jnp.where(row < limits_ref[2 * j + m : 2 * j + m + 1, :], outer[64 * m : 64 * m + 64], 0.0)
                        for m in range(2)
                    ],
                    axis=0,
                )
                edge_ref[j // 15] = edge.astype(BF16)
            outer = outer.astype(BF16)
            around = jnp.where(lo, tile(masked_ref, j + 2), tile(masked_ref, j))
            near = dot_t(
                jnp.concatenate([tile(masked_ref, j + 1), around], axis=1),
                jnp.concatenate([inner.astype(BF16), outer], axis=1),
            )
            field_ref[:, 128 * j : 128 * j + 128] = jnp.where(
                (lane & 63) < jnp.where(lane < 64, limits_ref[2 * j : 2 * j + 1, :], limits_ref[2 * j + 1 : 2 * j + 2, :]),
                near,
                0.0,
            )
    for g in range(0, 14, 2):
        raw = dot(collect, jnp.concatenate([nodes_ref[g], nodes_ref[g + 1]], axis=1))
        for n in range(2):
            plain_rows(raw[:, 128 * n : 128 * n + 128], node_raw.at[(g + n) % 4])
            node_rows[512 * (g + n) : 512 * (g + n) + 512, :] = node_raw[(g + n) % 4].astype(BF16)


def message_kernel(share_ref, one_ref, two_ref, three_ref, out_ref, cross_ref, sides_ref):
    total = share_ref[...].astype(F32)
    for ref in (one_ref, two_ref, three_ref):
        total = total + tile(ref, 16).astype(F32)
    packed = (total[:8] + total[8:]).astype(BF16)
    for n in range(64):
        out_ref[n] = packed
    sub = lax.axis_index("sub")
    cross_ref[...] = jnp.where(sub == 0, tile(three_ref, 18), tile(three_ref, 17))
    sides_ref[0] = jnp.where(sub == 2, tile(three_ref, 18), tile(one_ref, 18))
    sides_ref[1] = jnp.where(sub == 1, tile(three_ref, 17), tile(one_ref, 17))


def middle_kernel(
    node_coupling_hbm, links_vmem, node_links_hbm, coupling_hbm, rows_ref,
    own_ref, two_ref, three_ref, one_ref, near_ref, basis_ref, carry_rows,
    coupled_ref, field_ref, carry_ref, node_links_ref,
    links_ref, node_coupling_ref, coupling_ref, coeff_ref, picked_ref, spread_ref, sems,
):
    branch = lax.axis_index("leaf")
    own = [64 + branch, 32 + (branch >> 1), 16 + (branch >> 2), 8 + (branch >> 3)]
    sources = (own_ref, one_ref, two_ref, three_ref)
    copies = start_all(
        sems,
        [(links_vmem, links_ref)]
        + [(coupling_hbm.at[pl.ds(8 * n, 8)], coupling_ref.at[pl.ds(8 * n, 8)]) for n in range(4)]
        + [(node_coupling_hbm.at[:, own[n] >> 3], node_coupling_ref.at[n]) for n in range(4)]
        + [(node_links_hbm, node_links_ref)],
    )
    split = split_map()
    unit = jnp.where(iota((128, 128), 0) == iota((128, 128), 1), 1.0, 0.0).astype(BF16)
    for j in range(TILES):
        rows = carry_rows[64 * j : 64 * j + 64, :]
        turned = dot_t(unit, jnp.concatenate([rows, rows], axis=0))
        carry_ref[:, 128 * j : 128 * j + 128] = jnp.where(low_half(64), turned[:64], turned[64:]).astype(BF16)
    lo = low_half(16)
    nothing = jnp.zeros((16, 128), BF16)
    half = low_half(64)
    blank = jnp.zeros((64, 128), BF16)
    sub = lax.axis_index("sub")
    for d, ref in enumerate(sources):
        first = (sub ^ d) * 32
        for j in range(TILES):
            x = tile(ref, j)
            y = swap(x)
            for m, (a, b) in enumerate(((x, y), (y, x))):
                coeff_ref[0, first + 2 * j + m] = jnp.where(lo, a, nothing)
                coeff_ref[1, first + 2 * j + m] = jnp.where(lo, nothing, b)
    copies[0].wait()
    for leaf in range(32):
        for c in range(4):
            picked_ref[16 * leaf : 16 * leaf + 16, 128 * c : 128 * c + 128] = (
                coeff_ref[0, links_ref[2 * c, leaf] & 127]
                + coeff_ref[1, links_ref[2 * c + 1, leaf] & 127]
            )
    spread_ref[...] = dot(picked_ref[...], split).astype(BF16)
    for copy in copies[1:]:
        copy.wait()
    half = low_half(64)
    row, col = iota((64, 256), 0), iota((64, 256), 1)
    even = (iota((64, 128), 0) & 1) == 0

    def node(n):
        return rows_ref[pl.ds(pl.multiple_of((own[n] - 16) * 64, 64), 64), :]

    carried = [None, (node(0), None)]
    for n in (1, 2):
        high, low = carried[n]
        longer = dot(high[:, :64], node(n))
        if low is not None:
            longer = longer + dot(low[:, :64], node(n))
        carried.append(pieces(longer))
    lo192 = low_half(192)
    for n in range(4):
        pick = jnp.where(((row >> 1) == (col >> 3)) & ((col & 7) == (own[n] & 7)), 1.0, 0.0).astype(BF16)
        blocks = []
        for c in range(3):
            raw = dot(pick, node_coupling_ref[n, c])
            blocks.append(jnp.where(half == even, raw, swap(raw)))
        blocks = jnp.where(lo192, jnp.concatenate(blocks, axis=0), 0.0)
        if n == 0:
            rows = blocks
        else:
            blocks = blocks.astype(BF16)
            high, low = carried[n]
            full = dot_t(blocks, jnp.concatenate([high, high], axis=0))
            if low is not None:
                full = full + dot_t(blocks, jnp.concatenate([low, low], axis=0))
            upper = full.astype(BF16).astype(F32)
            rows = jnp.where(lo192, upper, full - upper)
        coupled_ref[256 * n : 256 * n + 192, :] = rows.astype(BF16)
        coupled_ref[256 * n + 192 : 256 * n + 256, :] = jnp.zeros((64, 128), BF16)

    for j in range(TILES):
        rows = spread_ref[32 * j : 32 * j + 32, :]
        both = dot(
            jnp.concatenate([rows[:, :256], rows[:, 256:]], axis=0),
            jnp.concatenate([coupling_ref[2 * j], coupling_ref[2 * j + 1]], axis=1),
        )
        a = jnp.concatenate([both[:16, :128], both[32:48, :128]], axis=0)
        b = jnp.concatenate([both[16:32, 128:], both[48:, 128:]], axis=0)
        far = jnp.where(lo, a[:16] + swap(a[16:]), swap(b[:16]) + b[16:]).astype(BF16)
        rows = basis_ref[64 * j : 64 * j + 64, :]
        blocks = jnp.concatenate([jnp.where(half, rows, blank), jnp.where(half, blank, rows)], axis=0)
        field_ref[:, 128 * j : 128 * j + 128] = tile(near_ref, j) + dot_t(far, blocks)


def downward_kernel(
    node_links_ref, sides_ref, cross_ref, message_ref,
    field_ref, carry_ref, edge_ref, nodes_ref, coupled_ref,
    out_hbm,
    table_ref, out_ref, sems,
):
    branch, sub = lax.axis_index("leaf"), lax.axis_index("sub")
    lo = low_half(16)
    lo8 = low_half(8)
    lo32 = low_half(32)

    zeros = jnp.zeros((16, 128), BF16)

    def weights(k):
        return nodes_ref[pl.ds(pl.multiple_of(128 * (k - 8), 128), 128), :]

    for q in range(32):
        one, two = message_ref[2 * q].astype(F32), message_ref[2 * q + 1].astype(F32)
        pair = jnp.concatenate(
            [jnp.where(lo8, one, swap(two)), jnp.where(lo8, swap(one), two)], axis=0
        )
        value = dot(pair.astype(BF16), nodes_ref[128 * (q + 24) : 128 * (q + 24) + 128, :])
        table_ref[q] = jnp.concatenate(pieces(value), axis=0)

    def leaf_node(k):
        one = message_ref[k - 64].astype(F32)
        other = swap(one)
        rows = jnp.concatenate([jnp.where(lo8, one, other), jnp.where(lo8, other, one)], axis=0)
        return jnp.concatenate([rows.astype(BF16), zeros], axis=0)

    def parent(k, children):
        value = dot(jnp.where(lo32, *children), weights(k))
        return jnp.concatenate(pieces(value[:16] + value[16:]), axis=0)

    ends = [[node_links_ref[m, (64 >> n) + (branch >> n)] for m in range(3)] for n in range(4)]
    sixteen = ends[2] + [2 * k + m for k in ends[3] for m in range(2)]
    values = [parent(k, [table_ref[2 * k - 32], table_ref[2 * k - 31]]) for k in sixteen]
    found = [
        [leaf_node(k) for k in ends[0]],
        [table_ref[k - 32] for k in ends[1]],
        values[:3],
        [parent(k, values[3 + 2 * n : 5 + 2 * n]) for n, k in enumerate(ends[3])],
    ]
    sources = []
    for a, b, c in found:
        sources += [jnp.where(lo32, a, b), c]
    down = dot(jnp.concatenate(sources, axis=1), coupled_ref[...])
    down = down[:16] + down[16:]
    down = (down + swap(down)).astype(BF16)
    shared = dot(down[:, :64], carry_ref[...])
    sent = []
    left = jnp.where(lo, zeros, jnp.where(sub == 0, cross_ref[...], sides_ref[0]))
    right = jnp.where(lo, jnp.where(sub == 3, cross_ref[...], sides_ref[1]), zeros)
    for j in range(TILES):
        out = shared[:, 128 * j : 128 * j + 128] + tile(field_ref, j)
        if j == 0:
            out = out + dot_t(left, edge_ref[0])
        if j == 15:
            out = out + dot_t(right, edge_ref[1])
        out_ref[:, 128 * j : 128 * j + 128] = out.astype(BF16)
        if j % 8 == 7:
            half = pl.ds(128 * (j - 7), 1024)
            sent.append(pltpu.make_async_copy(out_ref.at[:, half], out_hbm.at[:, half], sems.at[j // 8]))
            sent[-1].start()
    for copy in sent:
        copy.wait()


VMEM = pl.BlockSpec(memory_space=pltpu.VMEM)
HBM = pl.BlockSpec(memory_space=pltpu.HBM)
SMEM = pl.BlockSpec(memory_space=pltpu.SMEM)


def shape(dims, dtype=BF16):
    return jax.ShapeDtypeStruct(dims, dtype)


def pinned(dims, dtype=BF16):
    return pltpu.VMEM(dims, dtype)


def stays(x):
    return pltpu.with_memory_space_constraint(x, pltpu.HBM)


def near_by(x):
    return pltpu.with_memory_space_constraint(x, pltpu.VMEM)


def call(kernel, name, outs, in_specs, out_specs, scratch, size, mib, aliases={}):
    return pl.pallas_call(
        kernel,
        out_shape=outs,
        in_specs=in_specs,
        out_specs=out_specs,
        scratch_shapes=scratch,
        compiler_params=pltpu.CompilerParams(vmem_limit_bytes=mib << 20),
        cost_estimate=pl.CostEstimate(flops=10**9, bytes_accessed=size, transcendentals=0),
        input_output_aliases=aliases,
        name=name,
    )


def dma(count):
    return pltpu.SemaphoreType.DMA((count,))


def upward(*args):
    return call(
        upward_kernel, "upward",
        [
            shape((16, PAYLOAD)), pinned((16, 2048)), pinned((32, 128), I32), pinned((4, 256, 128)),
            pinned((4, 256, 128)), pinned((3, 4, 256, 128)), pinned((14, 256, 128)), pinned((8, 32), I32),
        ],
        [HBM] * 7, [VMEM] * 8,
        [
            pltpu.SMEM((32,), I32),
            pltpu.VMEM((16, 2048), BF16),
            pltpu.VMEM((512, 512), BF16),
            dma(7),
        ],
        10**6, 8,
    )(*args)


def near_field(*args):
    return call(
        near_kernel, "near",
        [
            pinned((16, 2048), F32), pinned((1024, 128)), pinned((1024, 128)), pinned((2, 128, 128)),
            pinned((16, 128)),
            pinned((56 * 128, 128)),
        ],
        [VMEM] * 7, [VMEM] * 6,
        [
            pltpu.VMEM((16, 18 * 128), BF16),
            pltpu.VMEM((8, 512, 128), F32),
            pltpu.VMEM((4, 512, 128), F32),
        ],
        3 * 10**6, 12,
    )(*args)


def message(*args):
    return call(
        message_kernel, "message", [shape((64, 8, 128)), shape((16, 128)), shape((2, 16, 128))], [VMEM] * 4, [VMEM] * 3, [],
        10**5, 4,
    )(*args)


def middle(*args):
    return call(
        middle_kernel, "middle",
        [pinned((1024, 128)), pinned((16, 2048), F32), pinned((64, 2048)), pltpu.SMEM((3, 128), I32)],
        [HBM, VMEM, HBM, HBM] + [VMEM] * 8, [VMEM] * 3 + [SMEM],
        [
            pltpu.SMEM((8, 32), I32),
            pltpu.VMEM((4, 3, 256, 128), BF16),
            pltpu.VMEM((32, 256, 128), BF16),
            pltpu.VMEM((2, 128, 16, 128), BF16),
            pltpu.VMEM((512, 512), BF16),
            pltpu.VMEM((512, 512), BF16),
            dma(10),
        ],
        6 * 10**6, 16, {9: 1},
    )(*args)


def downward(*args):
    return call(
        downward_kernel, "downward", shape((16, 2048)), [SMEM] + [VMEM] * 8, HBM,
        [pltpu.VMEM((32, 32, 128), BF16), pltpu.VMEM((16, 2048), BF16), dma(2)],
        4 * 10**6, 8,
    )(*args)


def grouped(table):
    lead, rows = table.shape[:-2], table.shape[-2]
    table = jnp.swapaxes(table.reshape(*lead, rows // 8, 8, 32, 128), -3, -2)
    return table.reshape(*lead, rows // 8, 256, 128)


def body(
    vectors, leaf_size, leaf_basis, near_blocks, leaf_links, leaf_coupling, leaf_transfer,
    node_transfer, node_links, node_coupling,
):
    basis, transfer, nodes = grouped(leaf_basis), grouped(leaf_transfer), grouped(node_transfer)
    coupling = grouped(leaf_coupling)[:, 0]
    near = grouped(near_blocks.transpose(1, 0, 2))
    node_coupled = grouped(node_coupling.transpose(1, 0, 2))

    basis, transfer, nodes, coupling, near, node_coupled, vectors, leaf_size, links, node_links = map(
        stays,
        (
            basis, transfer, nodes, coupling, near, node_coupled, vectors, leaf_size, leaf_links.T,
            node_links.T,
        ),
    )
    payload, *tables = upward(leaf_size, vectors, basis, transfer, near, nodes, links)
    kept_points, limits, basis, transfer, near, nodes, links = map(near_by, tables)
    others = [
        lax.ppermute(payload, "sub", [(s, s ^ d) for s in range(4)]) for d in (1, 2, 3)
    ]
    near_part, basis_p, carry, edge, share, nodes_p = near_field(
        kept_points, limits, near, basis, transfer, nodes, payload
    )
    messages, cross, sides = message(share, *others)
    summed = lax.all_to_all(messages, "leaf", 0, 0)

    branches = lax.axis_size("leaf")
    routes = [(4 * b, 4 * b + 4) for b in range(branches - 1)]
    routes += [(4 * b + 3, 4 * b - 1) for b in range(1, branches)]
    cross = lax.ppermute(cross, ("leaf", "sub"), routes)

    coupled, field, turned, partners = middle(
        node_coupled, links, node_links, coupling, near_by(nodes_p), payload, others[1], others[2], others[0],
        near_by(near_part), near_by(basis_p), near_by(carry),
    )
    return downward(
        pltpu.with_memory_space_constraint(partners, pltpu.SMEM), sides, cross, summed,
        *map(near_by, (field, turned, edge, nodes_p, coupled)),
    )


def solution(mesh):
    split = ("leaf", "sub")
    placed = (
        P(None, split), P(split), P(split, None), P(split, None, None), P(split, None),
        P(split, None, None), P(split, None), P(), P(), P(),
    )
    return jax.shard_map(
        body, mesh=mesh, in_specs=placed, out_specs=P(None, split), check_vma=False
    )
```
